256 devices in a mesh: dp: 16 (over y, x), tensor: 16 (over z, core).
Axes of the slice: x: 4, y: 4, z: 8, core: 2. Of those that a mesh axis runs over, the one named last changes fastest.
Arguments:
- buffer: bfloat16 [26624, 16384], P('dp', 'tensor'), may hold values from -1700 to 1700
- old_basis: bfloat16 [16384, 1024], P('tensor', 'dp'), may hold values from -0.046875 to 0.046875
Outputs:
- new_buffer: bfloat16 [26624, 16384], P('dp', 'tensor')
- weight_update: bfloat16 [26624, 16384], P('dp', 'tensor')
- new_basis: bfloat16 [16384, 1024], P('tensor', 'dp')
The draws below stay inside these ranges and needn't reach their ends.
All inputs are finite; a program needn't handle non-finite values.
Results may differ from the reference program's by a relative error of at most 0.015.
Values may be sent and summed in bfloat16 or wider, within the bound.
A program may use at most 128 MiB of HBM per device.

```python
import math
import jax
import jax.numpy as jnp
from jax import lax

ROWS = 26624
INPUTS = 16384
RANK = 1024


def draw_buffer(key, part):
    key = jax.random.fold_in(key, 11)
    streams = jax.random.split(key, 6)
    row_scale = jnp.exp(jax.random.uniform(streams[0], (ROWS, 1), jnp.float32, math.log(0.3), math.log(3.0)))
    col_scale = jnp.exp(jax.random.uniform(streams[1], (1, INPUTS), jnp.float32, math.log(0.3), math.log(3.0)))
    heavy_count = max(2, ROWS // 512)
    heavy_rows = jax.random.permutation(streams[5], ROWS)[:heavy_count]
    boost = jnp.ones((ROWS, 1), jnp.float32).at[heavy_rows, 0].set(30.0)
    values = jnp.clip(jax.random.normal(streams[2], (ROWS, INPUTS), jnp.float32), -4.0, 4.0)
    return (values * row_scale * col_scale * boost).astype(jnp.bfloat16)


def levels(own_key, dims, shards, least, top_value):
    def one(axis_at, blocks):
        heights = jax.random.uniform(jax.random.fold_in(jax.random.fold_in(own_key, 6), axis_at), (blocks,), jnp.float32, least / len(shards), top_value / len(shards))
        return jnp.repeat(jnp.exp(heights), dims[axis_at] // blocks).reshape((-1,) + (1,) * (len(dims) - axis_at - 1))

    loudness = one(*shards[0])
    for cut in shards[1:]:
        loudness = loudness * one(*cut)
    return loudness


def gaussian(stream_key, extent, scale, most, pieces=(), kind=jnp.bfloat16):
    array = jax.random.normal(stream_key, extent, jnp.float32) * scale
    if len(pieces) > 0:
        array = levels(stream_key, extent, pieces, -0.22, 0.18) * array
    return jnp.clip(array, min=-most, max=most).astype(kind)


def setup_inputs(seed: int = 0) -> dict:
    splits = jax.random.split(jax.random.key(seed), 3)
    buffer = draw_buffer(jax.random.fold_in(splits[2], 71), 0)
    old_basis = gaussian(splits[1], (INPUTS, RANK), INPUTS ** -0.5, 0.046875, ((0, 16), (1, 16)))
    return {"buffer": buffer, "old_basis": old_basis}


NORM_EPS = 1e-06
FEEDBACK_SHARE = 0.05

def reference(buffer, old_basis):
    projected = jnp.dot(buffer.astype(jnp.float32), old_basis.astype(jnp.float32), preferred_element_type=jnp.float32)
    gram = jnp.dot(projected.T.astype(jnp.float32), projected.astype(jnp.float32), precision=lax.Precision.HIGHEST, preferred_element_type=jnp.float32)
    factor_low = jnp.linalg.cholesky(gram)
    orthonormal = jax.scipy.linalg.solve_triangular(factor_low, projected.T, lower=True).T
    ortho_half = orthonormal.astype(jnp.bfloat16)
    transposed = jnp.dot(buffer.T.astype(jnp.float32), ortho_half.astype(jnp.float32), preferred_element_type=jnp.float32)
    squares = lax.optimization_barrier(jnp.sum(transposed * transposed, axis=0))
    trans_half = transposed.astype(jnp.bfloat16)
    new_basis = (trans_half.astype(jnp.float32) * lax.rsqrt(squares + NORM_EPS)).astype(jnp.bfloat16)
    feedback = jnp.dot(ortho_half.astype(jnp.float32), trans_half.T.astype(jnp.float32), preferred_element_type=jnp.float32)
    new_buffer = (buffer.astype(jnp.float32) - FEEDBACK_SHARE * feedback).astype(jnp.bfloat16)
    scale_up = math.sqrt(ROWS * INPUTS / RANK)
    weight_update = (-scale_up * jnp.dot(ortho_half.astype(jnp.float32), new_basis.T.astype(jnp.float32), preferred_element_type=jnp.float32)).astype(jnp.bfloat16)
    return (new_buffer, weight_update, new_basis)
```

```python
import math

import jax
import jax.numpy as jnp
from jax import lax
from jax.experimental import pallas as pl
from jax.experimental.pallas import tpu as pltpu
from jax.sharding import PartitionSpec as P

NORM_EPS = 1e-06
FEEDBACK_SHARE = 0.05
HI = lax.Precision.HIGHEST
F32 = jnp.float32
BF16 = jnp.bfloat16
NB = 128
MP = 16


def mm_tn(a, b, precision=None):
    return lax.dot_general(
        a, b, (((0,), (0,)), ((), ())), precision=precision, preferred_element_type=F32
    )


def mm_nn(a, b, precision=None):
    return lax.dot_general(
        a, b, (((1,), (0,)), ((), ())), precision=precision, preferred_element_type=F32
    )


def mm_nt(a, b, precision=None):
    return lax.dot_general(
        a, b, (((1,), (1,)), ((), ())), precision=precision, preferred_element_type=F32
    )


def eliminate_rows(rows, r0):
    lane = lax.broadcasted_iota(jnp.int32, (MP, NB), 1)
    row = lax.broadcasted_iota(jnp.int32, (MP, NB), 0)
    cols = [jnp.broadcast_to(rows[:, r0 + c : r0 + c + 1], (MP, NB)) for c in range(MP)]
    scale = jnp.zeros((MP, NB), F32)
    for c in range(MP):
        rs = lax.rsqrt(cols[c][c : c + 1, :])
        f = jnp.where(row > c, cols[c] * (rs * rs), 0.0)
        rows = jnp.where(lane == r0 + c, jnp.where(row == c, 1.0, 0.0), rows)
        for c2 in range(c + 1, MP):
            cols[c2] = cols[c2] - f * cols[c2][c : c + 1, :]
        rows = rows - f * rows[c : c + 1, :]
        scale = jnp.where(row == c, rs, scale)
    return rows * scale


def eliminate_block(block):
    lane = lax.broadcasted_iota(jnp.int32, (NB, NB), 1)
    for r0 in range(0, NB, MP):
        rows = eliminate_rows(block[r0 : r0 + MP, :], r0)
        block[r0 : r0 + MP, :] = rows
        if r0 + MP < NB:
            update = mm_tn(rows, rows, HI)[r0 + MP :, :]
            below = lane[r0 + MP :, :]
            old = jnp.where((below >= r0) & (below < r0 + MP), 0.0, block[r0 + MP :, :])
            block[r0 + MP :, :] = old - update


def chol_inv_kernel(g_ref, out_ref, block):
    n = g_ref.shape[0]
    nblk = n // NB
    out_ref[...] = g_ref[...]
    lane = lax.broadcasted_iota(jnp.int32, (NB, NB), 1)
    row = lax.broadcasted_iota(jnp.int32, (NB, NB), 0)

    def step(k, _):
        k0 = pl.multiple_of(k * NB, NB)
        block[...] = out_ref[pl.ds(k0, NB), pl.ds(k0, NB)]
        eliminate_block(block)
        linv = jnp.where(lane <= row, block[...], 0.0)
        out_ref[pl.ds(k0, NB), :] = mm_nn(linv, out_ref[pl.ds(k0, NB), :], HI)
        out_ref[pl.ds(k0, NB), pl.ds(k0, NB)] = linv

        def below(i, _):
            i0 = pl.multiple_of(i * NB, NB)
            u = out_ref[pl.ds(k0, NB), pl.ds(i0, NB)]
            out_ref[pl.ds(i0, NB), pl.ds(k0, NB)] = jnp.zeros((NB, NB), F32)
            out_ref[pl.ds(i0, NB), :] = out_ref[pl.ds(i0, NB), :] - mm_tn(
                u, out_ref[pl.ds(k0, NB), :], HI
            )
            return 0

        lax.fori_loop(k + 1, nblk, below, 0)
        return 0

    lax.fori_loop(0, nblk, step, 0)
    for k0 in range(0, n - NB, NB):
        out_ref[k0 : k0 + NB, k0 + NB :] = jnp.zeros((NB, n - k0 - NB), F32)


def chol_inv(g):
    n = g.shape[0]
    return pl.pallas_call(
        chol_inv_kernel,
        out_shape=jax.ShapeDtypeStruct((n, n), F32),
        in_specs=[pl.BlockSpec(memory_space=pltpu.VMEM)],
        out_specs=pl.BlockSpec(memory_space=pltpu.VMEM),
        scratch_shapes=[pltpu.VMEM((NB, NB), F32)],
        compiler_params=pltpu.CompilerParams(vmem_limit_bytes=40 << 20),
        cost_estimate=pl.CostEstimate(flops=60_000_000_000, bytes_accessed=8 << 20, transcendentals=0),
        name="chol_inv",
    )(g)


def rcopy(src, dst, send_sem, recv_sem, device):
    return pltpu.make_async_remote_copy(
        src_ref=src, dst_ref=dst, send_sem=send_sem, recv_sem=recv_sem,
        device_id=device, device_id_type=pl.DeviceIdType.MESH,
    )


def dp_steps(core):
    dp = lax.axis_index("dp")
    x, y = lax.rem(dp, 4), dp // 4

    def pairs(v):
        gray, high = lax.rem(v + v // 2, 2), v // 2
        near, far = v + 1 - 2 * lax.rem(v, 2), 3 - v
        other = 1 - core
        return (
            (other * near + core * far, other * gray + core * high),
            (other * far + core * near, other * high + core * gray),
        )

    xs = [(y * 4 + v, bit) for v, bit in pairs(x)]
    ys = [(v * 4 + x, bit) for v, bit in pairs(y)]
    return (xs + ys, ys + xs)


def enter(devices):
    barrier = pltpu.get_barrier_semaphore()
    for device in devices:
        pl.semaphore_signal(barrier, inc=1, device_id=device, device_id_type=pl.DeviceIdType.MESH)
    pl.semaphore_wait(barrier, len(devices))


def gram_kernel(p_ref, out_ref, part, half, got, sums, zgot, zsums, whole, core_send, core_recv, dp_send, dp_recv, z_send, z_recv, ag_send, ag_recv, zag_send, zag_recv):
    dp, tensor = lax.axis_index("dp"), lax.axis_index("tensor")
    core, z = lax.rem(tensor, 2), tensor // 2
    nz = lax.axis_size("tensor") // 2
    other = (dp, tensor + 1 - 2 * core)
    steps = dp_steps(core)
    zdev = [(dp, lax.rem(z + d, nz) * 2 + core) for d in range(nz)]
    enter([(partner, tensor) for partner, _ in steps[0]] + zdev[1:] + [other])

    n = p_ref.shape[1]
    nblk = n // NB
    at = 0
    for i in range(nblk):
        prod = mm_tn(p_ref[:, i * NB : (i + 1) * NB], p_ref[:, i * NB :], HI)
        for j in range(nblk - i):
            part[at : at + NB, :] = prod[:, j * NB : (j + 1) * NB]
            at += NB

    rows = at // 2
    mine = pl.multiple_of(core * rows, 8)
    theirs = pl.multiple_of((1 - core) * rows, 8)
    swap = rcopy(part.at[pl.ds(theirs, rows)], half, core_send.at[0], core_recv.at[0], other)
    swap.start()
    swap.wait_recv()
    half[...] = half[...] + part[pl.ds(mine, rows), :]

    length = rows // 2
    offs = [jnp.int32(0), jnp.int32(length)]
    trail = []
    pending = [swap]
    size = length
    got_at = 0
    for k in range(4):
        size //= 2
        copies = []
        for s in range(2):
            partner, bit = steps[s][k]
            keep = pl.multiple_of(offs[s] + bit * size, 8)
            give = pl.multiple_of(offs[s] + (1 - bit) * size, 8)
            copy = rcopy(half.at[pl.ds(give, size)], got.at[s, pl.ds(got_at, size)], dp_send.at[s, k], dp_recv.at[s, k], (partner, tensor))
            copy.start()
            copies.append(copy)
            offs[s] = keep
        for s in range(2):
            copies[s].wait_recv()
            half[pl.ds(offs[s], size), :] = half[pl.ds(offs[s], size), :] + got[s, pl.ds(got_at, size), :]
        trail.append((size, list(offs)))
        pending += copies
        got_at += size

    sums[0:size, :] = half[pl.ds(offs[0], size), :]
    sums[size : 2 * size, :] = half[pl.ds(offs[1], size), :]
    piece = sums.shape[0] // nz
    if sums.shape[0] > 2 * size:
        sums[2 * size :, :] = jnp.zeros((sums.shape[0] - 2 * size, NB), F32)
    copies = []
    for d in range(1, nz):
        zto = lax.rem(z + d, nz)
        copy = rcopy(sums.at[pl.ds(pl.multiple_of(zto * piece, 8), piece)], zgot.at[d], z_send.at[d], z_recv.at[d], zdev[d])
        copy.start()
        copies.append(copy)
    own = pl.multiple_of(z * piece, 8)
    total = sums[pl.ds(own, piece), :]
    for d in range(1, nz):
        copies[d - 1].wait_recv()
        total = total + zgot[d]
    pending += copies
    zsums[pl.ds(own, piece), :] = total
    copies = []
    for d in range(1, nz):
        copy = rcopy(zsums.at[pl.ds(own, piece)], zsums.at[pl.ds(own, piece)], zag_send.at[d], zag_recv.at[d], zdev[d])
        copy.start()
        copies.append(copy)
    for copy in copies:
        copy.wait_recv()
    pending += copies

    for s in range(2):
        whole[pl.ds(pl.multiple_of(mine + offs[s], 8), size), :] = zsums[s * size : (s + 1) * size, :]
    for k in reversed(range(4)):
        size, offs = trail[k]
        copies = []
        for s in range(2):
            region = whole.at[pl.ds(pl.multiple_of(mine + offs[s], 8), size)]
            copy = rcopy(region, region, ag_send.at[s, k], ag_recv.at[s, k], (steps[s][k][0], tensor))
            copy.start()
            copies.append(copy)
        for copy in copies:
            copy.wait_recv()
        pending += copies
    swap = rcopy(whole.at[pl.ds(mine, rows)], whole.at[pl.ds(mine, rows)], core_send.at[1], core_recv.at[1], other)
    swap.start()
    swap.wait_recv()
    pending.append(swap)
    at = 0
    for i in range(nblk):
        for j in range(nblk):
            if j < i:
                out_ref[i * NB : (i + 1) * NB, j * NB : (j + 1) * NB] = jnp.zeros((NB, NB), F32)
            else:
                out_ref[i * NB : (i + 1) * NB, j * NB : (j + 1) * NB] = whole[at : at + NB, :]
                at += NB
    for copy in pending:
        copy.wait_send()


def gram_sum(projected):
    n = projected.shape[1]
    nblk = n // NB
    packed = nblk * (nblk + 1) // 2 * NB
    nz = lax.axis_size("tensor") // 2
    rows = packed // 2
    last = rows // 2 // 16
    piece = -(-2 * last // (8 * nz)) * 8
    dma = pltpu.SemaphoreType.DMA
    return pl.pallas_call(
        gram_kernel,
        out_shape=jax.ShapeDtypeStruct((n, n), F32),
        in_specs=[pl.BlockSpec(memory_space=pltpu.VMEM)],
        out_specs=pl.BlockSpec(memory_space=pltpu.VMEM),
        scratch_shapes=[
            pltpu.VMEM((packed, NB), F32),
            pltpu.VMEM((rows, NB), F32),
            pltpu.VMEM((2, rows // 2, NB), F32),
            pltpu.VMEM((piece * nz, NB), F32),
            pltpu.VMEM((nz, piece, NB), F32),
            pltpu.VMEM((piece * nz, NB), F32),
            pltpu.VMEM((packed, NB), F32),
            dma((2,)), dma((2,)), dma((2, 4)), dma((2, 4)), dma((nz,)), dma((nz,)),
            dma((2, 4)), dma((2, 4)), dma((nz,)), dma((nz,)),
        ],
        compiler_params=pltpu.CompilerParams(
            vmem_limit_bytes=40 << 20, collective_id=1, has_side_effects=True
        ),
        cost_estimate=pl.CostEstimate(flops=30_000_000_000, bytes_accessed=8 << 20, transcendentals=0),
        name="gram_sum",
    )(projected)


def body(buffer, old_basis):
    full_basis = lax.all_gather(old_basis, "dp", axis=1, tiled=True)
    groups = lax.axis_size("tensor")
    rank = full_basis.shape[1]
    share = old_basis.shape[1]
    projected = lax.psum_scatter(
        mm_nn(buffer, full_basis), "tensor", scatter_dimension=0, tiled=True
    )
    gram = gram_sum(projected)

    proj_all = lax.all_gather(projected, "tensor", axis=0, tiled=True)
    proj_hi = lax.reduce_precision(proj_all, 8, 7)
    proj_lo = (proj_all - proj_hi).astype(BF16)
    mixed = mm_tn(buffer, proj_hi.astype(BF16)) + mm_tn(buffer, proj_lo)
    mixed = lax.psum_scatter(mixed, "dp", scatter_dimension=0, tiled=True)

    inverse = chol_inv(gram)
    trans = mm_nt(mixed, inverse, HI)
    squares = lax.psum(jnp.sum(trans * trans, axis=0), ("dp", "tensor"))
    trans_all = lax.all_gather(trans.astype(BF16), "dp", axis=0, tiled=True)
    ortho_all = mm_nt(proj_all, inverse, lax.Precision.HIGH).astype(BF16)
    basis_all = (trans_all.astype(F32) * lax.rsqrt(squares + NORM_EPS)).astype(BF16)
    new_basis = lax.dynamic_slice_in_dim(basis_all, lax.axis_index("dp") * share, share, axis=1)
    feedback = mm_nt(ortho_all, trans_all)
    new_buffer = (buffer.astype(F32) - FEEDBACK_SHARE * feedback).astype(BF16)
    scale_up = math.sqrt(
        buffer.shape[0] * lax.axis_size("dp") * buffer.shape[1] * groups / rank
    )
    product = mm_nt(ortho_all, basis_all)
    weight_update = (-scale_up * product).astype(BF16)
    return (new_buffer, weight_update, new_basis)


def solution(mesh):
    in_specs = (P("dp", "tensor"), P("tensor", "dp"))
    out_specs = (P("dp", "tensor"), P("dp", "tensor"), P("tensor", "dp"))
    return jax.shard_map(body, mesh=mesh, in_specs=in_specs, out_specs=out_specs, check_vma=False)
```

```python
import math

import jax
import jax.numpy as jnp
from jax import lax
from jax.experimental import pallas as pl
from jax.experimental.pallas import tpu as pltpu
from jax.sharding import PartitionSpec as P

NORM_EPS = 1e-06
FEEDBACK_SHARE = 0.05
HI = lax.Precision.HIGHEST
F32 = jnp.float32
BF16 = jnp.bfloat16
NB = 128
MP = 16


def mm_tn(a, b, precision=None):
    return lax.dot_general(
        a, b, (((0,), (0,)), ((), ())), precision=precision, preferred_element_type=F32
    )


def mm_nn(a, b, precision=None):
    return lax.dot_general(
        a, b, (((1,), (0,)), ((), ())), precision=precision, preferred_element_type=F32
    )


def mm_nt(a, b, precision=None):
    return lax.dot_general(
        a, b, (((1,), (1,)), ((), ())), precision=precision, preferred_element_type=F32
    )


def eliminate_rows(rows, r0):
    lane = lax.broadcasted_iota(jnp.int32, (MP, NB), 1)
    row = lax.broadcasted_iota(jnp.int32, (MP, NB), 0)
    cols = [jnp.broadcast_to(rows[:, r0 + c : r0 + c + 1], (MP, NB)) for c in range(MP)]
    scale = jnp.zeros((MP, NB), F32)
    for c in range(MP):
        rs = lax.rsqrt(cols[c][c : c + 1, :])
        f = jnp.where(row > c, cols[c] * (rs * rs), 0.0)
        rows = jnp.where(lane == r0 + c, jnp.where(row == c, 1.0, 0.0), rows)
        for c2 in range(c + 1, MP):
            cols[c2] = cols[c2] - f * cols[c2][c : c + 1, :]
        rows = rows - f * rows[c : c + 1, :]
        scale = jnp.where(row == c, rs, scale)
    return rows * scale


def eliminate_block(block):
    lane = lax.broadcasted_iota(jnp.int32, (NB, NB), 1)
    for r0 in range(0, NB, MP):
        rows = eliminate_rows(block[r0 : r0 + MP, :], r0)
        block[r0 : r0 + MP, :] = rows
        if r0 + MP < NB:
            update = mm_tn(rows, rows, HI)[r0 + MP :, :]
            below = lane[r0 + MP :, :]
            old = jnp.where((below >= r0) & (below < r0 + MP), 0.0, block[r0 + MP :, :])
            block[r0 + MP :, :] = old - update


def chol_inv_kernel(g_ref, out_ref, block):
    n = g_ref.shape[0]
    nblk = n // NB
    out_ref[...] = g_ref[...]
    lane = lax.broadcasted_iota(jnp.int32, (NB, NB), 1)
    row = lax.broadcasted_iota(jnp.int32, (NB, NB), 0)

    def step(k, _):
        k0 = pl.multiple_of(k * NB, NB)
        block[...] = out_ref[pl.ds(k0, NB), pl.ds(k0, NB)]
        eliminate_block(block)
        linv = jnp.where(lane <= row, block[...], 0.0)
        out_ref[pl.ds(k0, NB), :] = mm_nn(linv, out_ref[pl.ds(k0, NB), :], HI)
        out_ref[pl.ds(k0, NB), pl.ds(k0, NB)] = linv

        def below(i, _):
            i0 = pl.multiple_of(i * NB, NB)
            u = out_ref[pl.ds(k0, NB), pl.ds(i0, NB)]
            out_ref[pl.ds(i0, NB), pl.ds(k0, NB)] = jnp.zeros((NB, NB), F32)
            out_ref[pl.ds(i0, NB), :] = out_ref[pl.ds(i0, NB), :] - mm_tn(
                u, out_ref[pl.ds(k0, NB), :], HI
            )
            return 0

        lax.fori_loop(k + 1, nblk, below, 0)
        return 0

    lax.fori_loop(0, nblk, step, 0)
    for k0 in range(0, n - NB, NB):
        out_ref[k0 : k0 + NB, k0 + NB :] = jnp.zeros((NB, n - k0 - NB), F32)


def chol_inv(g):
    n = g.shape[0]
    return pl.pallas_call(
        chol_inv_kernel,
        out_shape=jax.ShapeDtypeStruct((n, n), F32),
        in_specs=[pl.BlockSpec(memory_space=pltpu.VMEM)],
        out_specs=pl.BlockSpec(memory_space=pltpu.VMEM),
        scratch_shapes=[pltpu.VMEM((NB, NB), F32)],
        compiler_params=pltpu.CompilerParams(vmem_limit_bytes=40 << 20),
        cost_estimate=pl.CostEstimate(flops=60_000_000_000, bytes_accessed=8 << 20, transcendentals=0),
        name="chol_inv",
    )(g)


def rcopy(src, dst, send_sem, recv_sem, device):
    return pltpu.make_async_remote_copy(
        src_ref=src, dst_ref=dst, send_sem=send_sem, recv_sem=recv_sem,
        device_id=device, device_id_type=pl.DeviceIdType.MESH,
    )


def dp_steps(core):
    dp = lax.axis_index("dp")
    x, y = lax.rem(dp, 4), dp // 4

    def pairs(v):
        gray, high = lax.rem(v + v // 2, 2), v // 2
        near, far = v + 1 - 2 * lax.rem(v, 2), 3 - v
        other = 1 - core
        return (
            (other * near + core * far, other * gray + core * high),
            (other * far + core * near, other * high + core * gray),
        )

    xs = [(y * 4 + v, bit) for v, bit in pairs(x)]
    ys = [(v * 4 + x, bit) for v, bit in pairs(y)]
    return (xs + ys, ys + xs)


def enter(devices):
    barrier = pltpu.get_barrier_semaphore()
    for device in devices:
        pl.semaphore_signal(barrier, inc=1, device_id=device, device_id_type=pl.DeviceIdType.MESH)
    pl.semaphore_wait(barrier, len(devices))


def gram_kernel(p_ref, out_ref, part, half, got, sums, zgot, zsums, whole, core_send, core_recv, dp_send, dp_recv, z_send, z_recv, ag_send, ag_recv, zag_send, zag_recv):
    dp, tensor = lax.axis_index("dp"), lax.axis_index("tensor")
    core, z = lax.rem(tensor, 2), tensor // 2
    nz = lax.axis_size("tensor") // 2
    other = (dp, tensor + 1 - 2 * core)
    steps = dp_steps(core)
    zdev = [(dp, lax.rem(z + d, nz) * 2 + core) for d in range(nz)]
    enter([(partner, tensor) for partner, _ in steps[0]] + zdev[1:] + [other])

    n = p_ref.shape[1]
    nblk = n // NB
    at = 0
    for i in range(nblk):
        prod = mm_tn(p_ref[:, i * NB : (i + 1) * NB], p_ref[:, i * NB :], HI)
        for j in range(nblk - i):
            part[at : at + NB, :] = prod[:, j * NB : (j + 1) * NB]
            at += NB

    rows = at // 2
    mine = pl.multiple_of(core * rows, 8)
    theirs = pl.multiple_of((1 - core) * rows, 8)
    swap = rcopy(part.at[pl.ds(theirs, rows)], half, core_send.at[0], core_recv.at[0], other)
    swap.start()
    swap.wait_recv()
    half[...] = half[...] + part[pl.ds(mine, rows), :]

    length = rows // 2
    offs = [jnp.int32(0), jnp.int32(length)]
    trail = []
    pending = [swap]
    size = length
    got_at = 0
    for k in range(4):
        size //= 2
        copies = []
        for s in range(2):
            partner, bit = steps[s][k]
            keep = pl.multiple_of(offs[s] + bit * size, 8)
            give = pl.multiple_of(offs[s] + (1 - bit) * size, 8)
            copy = rcopy(half.at[pl.ds(give, size)], got.at[s, pl.ds(got_at, size)], dp_send.at[s, k], dp_recv.at[s, k], (partner, tensor))
            copy.start()
            copies.append(copy)
            offs[s] = keep
        for s in range(2):
            copies[s].wait_recv()
            half[pl.ds(offs[s], size), :] = half[pl.ds(offs[s], size), :] + got[s, pl.ds(got_at, size), :]
        trail.append((size, list(offs)))
        pending += copies
        got_at += size

    sums[0:size, :] = half[pl.ds(offs[0], size), :]
    sums[size : 2 * size, :] = half[pl.ds(offs[1], size), :]
    piece = sums.shape[0] // nz
    if sums.shape[0] > 2 * size:
        sums[2 * size :, :] = jnp.zeros((sums.shape[0] - 2 * size, NB), F32)
    copies = []
    for d in range(1, nz):
        zto = lax.rem(z + d, nz)
        copy = rcopy(sums.at[pl.ds(pl.multiple_of(zto * piece, 8), piece)], zgot.at[d], z_send.at[d], z_recv.at[d], zdev[d])
        copy.start()
        copies.append(copy)
    own = pl.multiple_of(z * piece, 8)
    total = sums[pl.ds(own, piece), :]
    for d in range(1, nz):
        copies[d - 1].wait_recv()
        total = total + zgot[d]
    pending += copies
    zsums[pl.ds(own, piece), :] = total
    copies = []
    for d in range(1, nz):
        copy = rcopy(zsums.at[pl.ds(own, piece)], zsums.at[pl.ds(own, piece)], zag_send.at[d], zag_recv.at[d], zdev[d])
        copy.start()
        copies.append(copy)
    for copy in copies:
        copy.wait_recv()
    pending += copies

    for s in range(2):
        whole[pl.ds(pl.multiple_of(mine + offs[s], 8), size), :] = zsums[s * size : (s + 1) * size, :]
    for k in reversed(range(4)):
        size, offs = trail[k]
        copies = []
        for s in range(2):
            region = whole.at[pl.ds(pl.multiple_of(mine + offs[s], 8), size)]
            copy = rcopy(region, region, ag_send.at[s, k], ag_recv.at[s, k], (steps[s][k][0], tensor))
            copy.start()
            copies.append(copy)
        for copy in copies:
            copy.wait_recv()
        pending += copies
    swap = rcopy(whole.at[pl.ds(mine, rows)], whole.at[pl.ds(mine, rows)], core_send.at[1], core_recv.at[1], other)
    swap.start()
    swap.wait_recv()
    pending.append(swap)
    at = 0
    for i in range(nblk):
        for j in range(nblk):
            if j < i:
                out_ref[i * NB : (i + 1) * NB, j * NB : (j + 1) * NB] = jnp.zeros((NB, NB), F32)
            else:
                out_ref[i * NB : (i + 1) * NB, j * NB : (j + 1) * NB] = whole[at : at + NB, :]
                at += NB
    for copy in pending:
        copy.wait_send()


def gram_sum(projected):
    n = projected.shape[1]
    nblk = n // NB
    packed = nblk * (nblk + 1) // 2 * NB
    nz = lax.axis_size("tensor") // 2
    rows = packed // 2
    last = rows // 2 // 16
    piece = -(-2 * last // (8 * nz)) * 8
    dma = pltpu.SemaphoreType.DMA
    return pl.pallas_call(
        gram_kernel,
        out_shape=jax.ShapeDtypeStruct((n, n), F32),
        in_specs=[pl.BlockSpec(memory_space=pltpu.VMEM)],
        out_specs=pl.BlockSpec(memory_space=pltpu.VMEM),
        scratch_shapes=[
            pltpu.VMEM((packed, NB), F32),
            pltpu.VMEM((rows, NB), F32),
            pltpu.VMEM((2, rows // 2, NB), F32),
            pltpu.VMEM((piece * nz, NB), F32),
            pltpu.VMEM((nz, piece, NB), F32),
            pltpu.VMEM((piece * nz, NB), F32),
            pltpu.VMEM((packed, NB), F32),
            dma((2,)), dma((2,)), dma((2, 4)), dma((2, 4)), dma((nz,)), dma((nz,)),
            dma((2, 4)), dma((2, 4)), dma((nz,)), dma((nz,)),
        ],
        compiler_params=pltpu.CompilerParams(
            vmem_limit_bytes=40 << 20, collective_id=1, has_side_effects=True
        ),
        cost_estimate=pl.CostEstimate(flops=30_000_000_000, bytes_accessed=8 << 20, transcendentals=0),
        name="gram_sum",
    )(projected)


def dp_offsets(dp, core, length):
    def bits(v):
        gray, high = lax.rem(v + v // 2, 2), v // 2
        other = 1 - core
        return [other * gray + core * high, other * high + core * gray]

    xs, ys = bits(lax.rem(dp, 4)), bits(dp // 4)
    out = []
    for order in (xs + ys, ys + xs):
        at, size = 0, length
        for bit in order:
            size //= 2
            at = at + bit * size
        out.append(at)
    return out


def finish_kernel(mixed_ref, inv_ref, proj_ref, ortho_ref, trans_ref, basis_ref, inv_hi, inv_lo, stacked, whole, sq, sq_t, sq_d, sq_sum, ag_send, ag_recv, t_send, t_recv, d_send, d_recv):
    dp, tensor = lax.axis_index("dp"), lax.axis_index("tensor")
    ndp, ntensor = lax.axis_size("dp"), lax.axis_size("tensor")
    core = lax.rem(tensor, 2)
    steps = dp_steps(core)
    tdev = [(dp, lax.rem(tensor + d, ntensor)) for d in range(ntensor)]
    ddev = [(lax.rem(dp + d, ndp), tensor) for d in range(ndp)]
    enter(tdev[1:] + ddev[1:])

    n = inv_ref.shape[0]
    for k in range(0, n, 256):
        wide = inv_ref[k : k + 256, :]
        high = wide.astype(BF16)
        inv_hi[k : k + 256, :] = high
        inv_lo[k : k + 256, :] = (wide - high.astype(F32)).astype(BF16)
    share = mixed_ref.shape[0]
    high = mixed_ref[...].astype(BF16)
    stacked[0:share, :] = high
    stacked[share:, :] = (mixed_ref[...] - high.astype(F32)).astype(BF16)
    length = whole.shape[0] // 2
    offs = dp_offsets(dp, core, length)
    spots = [pl.multiple_of(s * length + offs[s], 16) for s in range(2)]
    for k in range(0, n, 256):
        both = mm_nt(stacked[...], inv_hi[k : k + 256, :])
        part = both[0:share, :] + both[share:, :] + mm_nt(stacked[0:share, :], inv_lo[k : k + 256, :])
        squares = jnp.sum(part * part, axis=0, keepdims=True)
        for j in range(0, 256, NB):
            sq[(k + j) // NB : (k + j) // NB + 1, :] = squares[:, j : j + NB]
        part = part.astype(BF16)
        for s in range(2):
            whole[pl.ds(spots[s], share // 2), k : k + 256] = part[s * share // 2 : (s + 1) * share // 2, :]

    pending = []

    def gather_step(k):
        size = length >> (k + 1)
        copies = []
        for s in range(2):
            start = s * length + offs[s] // size * size
            region = whole.at[pl.ds(pl.multiple_of(start, 16), size)]
            copy = rcopy(region, region, ag_send.at[s, k], ag_recv.at[s, k], (steps[s][k][0], tensor))
            copy.start()
            copies.append(copy)
        pending.extend(copies)
        return copies

    def spread(source, slots, send, recv, devices):
        copies = []
        for d in range(1, len(devices)):
            copy = rcopy(source, slots.at[d], send.at[d], recv.at[d], devices[d])
            copy.start()
            copies.append(copy)
        pending.extend(copies)
        return copies

    def total(source, slots, copies):
        out = source[...]
        for d in range(1, slots.shape[0]):
            copies[d - 1].wait_recv()
            out = out + slots[d]
        return out

    def ortho_part(i):
        rows = proj_ref.shape[0] // 4
        rows0 = i * rows
        wide = proj_ref[rows0 : rows0 + rows, :]
        high = wide.astype(BF16)
        low = (wide - high.astype(F32)).astype(BF16)
        for k in range(0, n, 256):
            e = k + 256
            hi, lo = inv_hi[k:e, 0:e], inv_lo[k:e, 0:e]
            value = mm_nt(high[:, 0:e], hi) + (mm_nt(low[:, 0:e], hi) + mm_nt(high[:, 0:e], lo))
            ortho_ref[rows0 : rows0 + rows, k:e] = value.astype(BF16)

    across = spread(sq, sq_t, t_send, t_recv, tdev)
    copies = gather_step(3)
    ortho_part(0)
    sq_sum[...] = total(sq, sq_t, across)
    down = spread(sq_sum, sq_d, d_send, d_recv, ddev)
    for i, k in enumerate((2, 1, 0)):
        for copy in copies:
            copy.wait_recv()
        copies = gather_step(k)
        ortho_part(i + 1)
    scale = lax.rsqrt(total(sq_sum, sq_d, down) + NORM_EPS)
    for copy in copies:
        copy.wait_recv()
    half = share // 2
    for d in range(ndp):
        there = dp_offsets(jnp.int32(d), core, length)
        for s in range(2):
            rows0 = d * share + s * half
            block = whole[pl.ds(pl.multiple_of(s * length + there[s], 16), half), :]
            trans_ref[rows0 : rows0 + half, :] = block
            for j in range(n // NB):
                basis_ref[rows0 : rows0 + half, j * NB : (j + 1) * NB] = (
                    block[:, j * NB : (j + 1) * NB].astype(F32) * scale[j : j + 1, :]
                ).astype(BF16)
    for copy in pending:
        copy.wait_send()


def finish(mixed, inverse, proj_all):
    share, n = mixed.shape
    rows = proj_all.shape[0]
    ndp, ntensor = lax.axis_size("dp"), lax.axis_size("tensor")
    dma = pltpu.SemaphoreType.DMA
    vmem = pl.BlockSpec(memory_space=pltpu.VMEM)
    return pl.pallas_call(
        finish_kernel,
        out_shape=[
            jax.ShapeDtypeStruct((rows, n), BF16),
            jax.ShapeDtypeStruct((share * ndp, n), BF16),
            jax.ShapeDtypeStruct((share * ndp, n), BF16),
        ],
        in_specs=[vmem] * 3,
        out_specs=[vmem] * 3,
        scratch_shapes=[
            pltpu.VMEM((n, n), BF16), pltpu.VMEM((n, n), BF16),
            pltpu.VMEM((2 * share, n), BF16), pltpu.VMEM((share * ndp, n), BF16),
            pltpu.VMEM((n // NB, NB), F32), pltpu.VMEM((ntensor, n // NB, NB), F32),
            pltpu.VMEM((ndp, n // NB, NB), F32), pltpu.VMEM((n // NB, NB), F32),
            dma((2, 4)), dma((2, 4)), dma((ntensor,)), dma((ntensor,)), dma((ndp,)), dma((ndp,)),
        ],
        compiler_params=pltpu.CompilerParams(
            vmem_limit_bytes=48 << 20, collective_id=2, has_side_effects=True
        ),
        cost_estimate=pl.CostEstimate(flops=20_000_000_000, bytes_accessed=16 << 20, transcendentals=0),
        name="finish",
    )(mixed, inverse, proj_all)


def project_kernel(buf_ref, share_ref, out_ref, basis, natural, part, swapped, acc, ring, ag_send, ag_recv, sw_send, sw_recv, ring_send, ring_recv):
    dp, tensor = lax.axis_index("dp"), lax.axis_index("tensor")
    ndp, nz = lax.axis_size("dp"), lax.axis_size("tensor") // 2
    core, z = lax.rem(tensor, 2), tensor // 2
    other = (dp, tensor + 1 - 2 * core)
    after = (dp, lax.rem(z + 1 - 2 * core + nz, nz) * 2 + core)
    before = (dp, lax.rem(z - 1 + 2 * core + nz, nz) * 2 + core)
    steps = dp_steps(core)
    enter([(partner, tensor) for partner, _ in steps[0]] + [other, after, before])
    pending = []

    share = share_ref.shape[0]
    length = basis.shape[0] // 2
    offs = dp_offsets(dp, core, length)
    half = share // 2
    for s in range(2):
        basis[pl.ds(pl.multiple_of(s * length + offs[s], 16), half), :] = share_ref[s * half : (s + 1) * half, :]
    for k in reversed(range(4)):
        size = length >> (k + 1)
        copies = []
        for s in range(2):
            region = basis.at[pl.ds(pl.multiple_of(s * length + offs[s] // size * size, 16), size)]
            copy = rcopy(region, region, ag_send.at[s, k], ag_recv.at[s, k], (steps[s][k][0], tensor))
            copy.start()
            copies.append(copy)
        for copy in copies:
            copy.wait_recv()
        pending += copies
    for d in range(ndp):
        there = dp_offsets(jnp.int32(d), core, length)
        for s in range(2):
            rows0 = d * share + s * half
            natural[rows0 : rows0 + half, :] = basis[pl.ds(pl.multiple_of(s * length + there[s], 16), half), :]

    chunk = buf_ref.shape[0] // nz
    rows = chunk // 2
    mine = pl.multiple_of(core * rows, 8)
    theirs = pl.multiple_of((1 - core) * rows, 8)

    def compute(r):
        rows0 = pl.multiple_of(lax.rem(z + r, nz) * chunk, 16)
        for k in range(0, natural.shape[0], 512):
            part[r, :, k : k + 512] = mm_nt(buf_ref[pl.ds(rows0, chunk), :], natural[k : k + 512, :])
        copy = rcopy(part.at[r, pl.ds(theirs, rows)], swapped.at[r], sw_send.at[r], sw_recv.at[r], other)
        copy.start()
        pending.append(copy)

    columns = out_ref.shape[1] // 2

    def term(r, h):
        return part[r, pl.ds(mine, rows), h * columns : (h + 1) * columns] + swapped[r, :, h * columns : (h + 1) * columns]

    def swap_wait(r):
        rcopy(part.at[r, pl.ds(theirs, rows)], swapped.at[r], sw_send.at[r], sw_recv.at[r], other).wait_recv()

    last = [None, None]

    def ring_step(s):
        r = core * (1 + s) + (1 - core) * (nz - 1 - s)
        swap_wait(r)
        for h in range(2):
            value = term(r, h)
            if s > 0:
                last[h].wait_recv()
                value = value + ring[s - 1, h]
            acc[s, h] = value
            last[h] = rcopy(acc.at[s, h], ring.at[s, h], ring_send.at[s, h], ring_recv.at[s, h], after)
            last[h].start()
            pending.append(last[h])

    order = []
    for r in range(1, nz // 2):
        order += [r, nz - r]
    order += [nz // 2, 0]
    done = 0
    for i in range(0, nz, 2):
        compute(order[i])
        compute(order[i + 1])
        if i >= 2:
            ring_step(done)
            done += 1
    for s in range(done, nz - 1):
        ring_step(s)
    swap_wait(0)
    for h in range(2):
        value = term(0, h)
        last[h].wait_recv()
        out_ref[:, h * columns : (h + 1) * columns] = value + ring[nz - 2, h]
    for copy in pending:
        copy.wait_send()


def project(buffer, share):
    nz = lax.axis_size("tensor") // 2
    n = share.shape[0] * lax.axis_size("dp")
    depth = share.shape[1]
    rows = buffer.shape[0] // nz // 2
    dma = pltpu.SemaphoreType.DMA
    vmem = pl.BlockSpec(memory_space=pltpu.VMEM)
    return pl.pallas_call(
        project_kernel,
        out_shape=jax.ShapeDtypeStruct((rows, n), F32),
        in_specs=[vmem] * 2,
        out_specs=vmem,
        scratch_shapes=[
            pltpu.VMEM((n, depth), BF16), pltpu.VMEM((n, depth), BF16),
            pltpu.VMEM((nz, 2 * rows, n), F32), pltpu.VMEM((nz, rows, n), F32),
            pltpu.VMEM((nz - 1, 2, rows, n // 2), F32), pltpu.VMEM((nz - 1, 2, rows, n // 2), F32),
            dma((2, 4)), dma((2, 4)), dma((nz,)), dma((nz,)), dma((nz - 1, 2)), dma((nz - 1, 2)),
        ],
        compiler_params=pltpu.CompilerParams(
            vmem_limit_bytes=48 << 20, collective_id=3, has_side_effects=True
        ),
        cost_estimate=pl.CostEstimate(flops=20_000_000_000, bytes_accessed=16 << 20, transcendentals=0),
        name="project",
    )(buffer, share)


def body(buffer, old_basis):
    groups = lax.axis_size("tensor")
    share = old_basis.shape[1]
    rank = share * lax.axis_size("dp")
    projected = project(buffer, old_basis.T)
    gram = gram_sum(projected)

    proj_all = lax.all_gather(projected, "tensor", axis=0, tiled=True)
    proj_hi = lax.reduce_precision(proj_all, 8, 7)
    proj_lo = (proj_all - proj_hi).astype(BF16)
    mixed = mm_tn(buffer, proj_hi.astype(BF16)) + mm_tn(buffer, proj_lo)
    mixed = lax.psum_scatter(mixed, "dp", scatter_dimension=0, tiled=True)

    inverse = chol_inv(gram)
    ortho_all, trans_all, basis_all = finish(mixed, inverse, proj_all)
    new_basis = lax.dynamic_slice_in_dim(basis_all, lax.axis_index("dp") * share, share, axis=1)
    feedback = mm_nt(ortho_all, trans_all)
    new_buffer = (buffer.astype(F32) - FEEDBACK_SHARE * feedback).astype(BF16)
    scale_up = math.sqrt(
        buffer.shape[0] * lax.axis_size("dp") * buffer.shape[1] * groups / rank
    )
    product = mm_nt(ortho_all, basis_all)
    weight_update = (-scale_up * product).astype(BF16)
    return (new_buffer, weight_update, new_basis)


def solution(mesh):
    in_specs = (P("dp", "tensor"), P("tensor", "dp"))
    out_specs = (P("dp", "tensor"), P("dp", "tensor"), P("tensor", "dp"))
    return jax.shard_map(body, mesh=mesh, in_specs=in_specs, out_specs=out_specs, check_vma=False)
```

```python
import math

import jax
import jax.numpy as jnp
from jax import lax
from jax.experimental import pallas as pl
from jax.experimental.pallas import tpu as pltpu
from jax.sharding import PartitionSpec as P

NORM_EPS = 1e-06
FEEDBACK_SHARE = 0.05
HI = lax.Precision.HIGHEST
F32 = jnp.float32
BF16 = jnp.bfloat16
NB = 128
MP = 16


def mm_tn(a, b, precision=None):
    return lax.dot_general(
        a, b, (((0,), (0,)), ((), ())), precision=precision, preferred_element_type=F32
    )


def mm_nn(a, b, precision=None):
    return lax.dot_general(
        a, b, (((1,), (0,)), ((), ())), precision=precision, preferred_element_type=F32
    )


def mm_nt(a, b, precision=None):
    return lax.dot_general(
        a, b, (((1,), (1,)), ((), ())), precision=precision, preferred_element_type=F32
    )


def eliminate_rows(rows, r0):
    lane = lax.broadcasted_iota(jnp.int32, (MP, NB), 1)
    row = lax.broadcasted_iota(jnp.int32, (MP, NB), 0)
    cols = [jnp.broadcast_to(rows[:, r0 + c : r0 + c + 1], (MP, NB)) for c in range(MP)]
    scale = jnp.zeros((MP, NB), F32)
    for c in range(MP):
        rs = lax.rsqrt(cols[c][c : c + 1, :])
        f = jnp.where(row > c, cols[c] * (rs * rs), 0.0)
        rows = jnp.where(lane == r0 + c, jnp.where(row == c, 1.0, 0.0), rows)
        for c2 in range(c + 1, MP):
            cols[c2] = cols[c2] - f * cols[c2][c : c + 1, :]
        rows = rows - f * rows[c : c + 1, :]
        scale = jnp.where(row == c, rs, scale)
    return rows * scale


def eliminate_block(block):
    lane = lax.broadcasted_iota(jnp.int32, (NB, NB), 1)
    for r0 in range(0, NB, MP):
        rows = eliminate_rows(block[r0 : r0 + MP, :], r0)
        block[r0 : r0 + MP, :] = rows
        if r0 + MP < NB:
            update = mm_tn(rows, rows, HI)[r0 + MP :, :]
            below = lane[r0 + MP :, :]
            old = jnp.where((below >= r0) & (below < r0 + MP), 0.0, block[r0 + MP :, :])
            block[r0 + MP :, :] = old - update


def chol_inv(out_ref, block, between):
    n = out_ref.shape[0]
    nblk = n // NB
    lane = lax.broadcasted_iota(jnp.int32, (NB, NB), 1)
    row = lax.broadcasted_iota(jnp.int32, (NB, NB), 0)

    def step(k, _):
        between(k)
        k0 = pl.multiple_of(k * NB, NB)
        block[...] = out_ref[pl.ds(k0, NB), pl.ds(k0, NB)]
        eliminate_block(block)
        linv = jnp.where(lane <= row, block[...], 0.0)
        out_ref[pl.ds(k0, NB), :] = mm_nn(linv, out_ref[pl.ds(k0, NB), :], HI)
        out_ref[pl.ds(k0, NB), pl.ds(k0, NB)] = linv

        def below(i, _):
            i0 = pl.multiple_of(i * NB, NB)
            u = out_ref[pl.ds(k0, NB), pl.ds(i0, NB)]
            out_ref[pl.ds(i0, NB), pl.ds(k0, NB)] = jnp.zeros((NB, NB), F32)
            out_ref[pl.ds(i0, NB), :] = out_ref[pl.ds(i0, NB), :] - mm_tn(
                u, out_ref[pl.ds(k0, NB), :], HI
            )
            return 0

        lax.fori_loop(k + 1, nblk, below, 0)
        return 0

    lax.fori_loop(0, nblk, step, 0)
    for k0 in range(0, n - NB, NB):
        out_ref[k0 : k0 + NB, k0 + NB :] = jnp.zeros((NB, n - k0 - NB), F32)


def rcopy(src, dst, send_sem, recv_sem, device):
    return pltpu.make_async_remote_copy(
        src_ref=src, dst_ref=dst, send_sem=send_sem, recv_sem=recv_sem,
        device_id=device, device_id_type=pl.DeviceIdType.MESH,
    )


def dp_steps(core):
    dp = lax.axis_index("dp")
    x, y = lax.rem(dp, 4), dp // 4

    def pairs(v):
        gray, high = lax.rem(v + v // 2, 2), v // 2
        near, far = v + 1 - 2 * lax.rem(v, 2), 3 - v
        other = 1 - core
        return (
            (other * near + core * far, other * gray + core * high),
            (other * far + core * near, other * high + core * gray),
        )

    xs = [(y * 4 + v, bit) for v, bit in pairs(x)]
    ys = [(v * 4 + x, bit) for v, bit in pairs(y)]
    return (xs + ys, ys + xs)


def enter(devices):
    barrier = pltpu.get_barrier_semaphore()
    for device in devices:
        pl.semaphore_signal(barrier, inc=1, device_id=device, device_id_type=pl.DeviceIdType.MESH)
    pl.semaphore_wait(barrier, len(devices))


def factor_kernel(p_ref, buf_ref, inv_ref, mixed_ref, all_ref, part, half, got, sums, zgot, zsums, whole, block, mixed, mixed_got, core_send, core_recv, dp_send, dp_recv, z_send, z_recv, ag_send, ag_recv, zag_send, zag_recv, plus_send, plus_recv, minus_send, minus_recv, pair_send, pair_recv, w_send, w_recv):
    dp, tensor = lax.axis_index("dp"), lax.axis_index("tensor")
    core, z = lax.rem(tensor, 2), tensor // 2
    nz = lax.axis_size("tensor") // 2
    other = (dp, tensor + 1 - 2 * core)
    steps = dp_steps(core)
    zdev = [(dp, lax.rem(z + d, nz) * 2 + core) for d in range(nz)]
    enter([(partner, tensor) for partner, _ in steps[0]] + zdev[1:] + [other])
    pending = []

    prows, n = p_ref.shape

    def region(r, c):
        at = (lax.rem(z + r, nz) * 2 + c) * prows
        return all_ref.at[pl.ds(pl.multiple_of(at, 8), prows)]

    def begin(copy):
        copy.start()
        pending.append(copy)
        return copy

    def pass_on(j):
        plus = region(nz - j if j else 0, core)
        begin(rcopy(plus, plus, plus_send.at[j], plus_recv.at[j], zdev[1]))
        if j < nz // 2 - 1:
            minus = region(j, core)
            begin(rcopy(minus, minus, minus_send.at[j], minus_recv.at[j], zdev[nz - 1]))

    def across(r):
        here = region(r, core)
        begin(rcopy(here, here, pair_send.at[r], pair_recv.at[r], other))

    def poll(j):
        here = region(nz - j, core)
        rcopy(here, here, plus_send.at[j - 1], plus_recv.at[j - 1], zdev[1]).wait_recv()
        if j < nz // 2:
            here = region(j, core)
            rcopy(here, here, minus_send.at[j - 1], minus_recv.at[j - 1], zdev[nz - 1]).wait_recv()
            pass_on(j)
            across(j)
        across(nz - j)

    chunk = 2 * prows

    def accumulate(r):
        here = region(r, core)
        rcopy(here, here, pair_send.at[r], pair_recv.at[r], other).wait_recv()
        rows0 = pl.multiple_of(lax.rem(z + r, nz) * chunk, 16)
        wide = all_ref[pl.ds(rows0, chunk), :]
        high = wide.astype(BF16)
        low = (wide - high.astype(F32)).astype(BF16)

        def strip(i, _):
            i0 = pl.multiple_of(i * 256, 256)
            left = buf_ref[pl.ds(rows0, chunk), pl.ds(i0, 256)]
            for k in range(0, n, 256):
                value = mm_tn(left, high[:, k : k + 256]) + mm_tn(left, low[:, k : k + 256])
                if r:
                    value = value + mixed[pl.ds(i0, 256), k : k + 256]
                mixed[pl.ds(i0, 256), k : k + 256] = value
            return 0

        lax.fori_loop(0, mixed.shape[0] // 256, strip, 0)

    own_rows = pl.multiple_of(tensor * prows, 8)
    all_ref[pl.ds(own_rows, prows), :] = p_ref[...]
    pass_on(0)
    across(0)

    nblk = n // NB
    at = 0
    for i in range(nblk):
        prod = mm_tn(p_ref[:, i * NB : (i + 1) * NB], p_ref[:, i * NB :], HI)
        for j in range(nblk - i):
            part[at : at + NB, :] = prod[:, j * NB : (j + 1) * NB]
            at += NB

    rows = at // 2
    mine = pl.multiple_of(core * rows, 8)
    theirs = pl.multiple_of((1 - core) * rows, 8)
    swap = begin(rcopy(part.at[pl.ds(theirs, rows)], half, core_send.at[0], core_recv.at[0], other))
    swap.wait_recv()
    half[...] = half[...] + part[pl.ds(mine, rows), :]

    length = rows // 2
    offs = [jnp.int32(0), jnp.int32(length)]
    trail = []
    size = length
    got_at = 0
    for k in range(4):
        size //= 2
        copies = []
        for s in range(2):
            partner, bit = steps[s][k]
            keep = pl.multiple_of(offs[s] + bit * size, 8)
            give = pl.multiple_of(offs[s] + (1 - bit) * size, 8)
            copies.append(begin(rcopy(half.at[pl.ds(give, size)], got.at[s, pl.ds(got_at, size)], dp_send.at[s, k], dp_recv.at[s, k], (partner, tensor))))
            offs[s] = keep
        if k == 0:
            accumulate(0)
        elif k >= 2:
            accumulate((1, nz - 1)[k - 2])
        for s in range(2):
            copies[s].wait_recv()
            half[pl.ds(offs[s], size), :] = half[pl.ds(offs[s], size), :] + got[s, pl.ds(got_at, size), :]
        if k == 0:
            poll(1)
        trail.append((size, list(offs)))
        got_at += size

    sums[0:size, :] = half[pl.ds(offs[0], size), :]
    sums[size : 2 * size, :] = half[pl.ds(offs[1], size), :]
    piece = sums.shape[0] // nz
    if sums.shape[0] > 2 * size:
        sums[2 * size :, :] = jnp.zeros((sums.shape[0] - 2 * size, NB), F32)
    copies = []
    for d in range(1, nz):
        zto = lax.rem(z + d, nz)
        copies.append(begin(rcopy(sums.at[pl.ds(pl.multiple_of(zto * piece, 8), piece)], zgot.at[d], z_send.at[d], z_recv.at[d], zdev[d])))
    poll(2)
    own = pl.multiple_of(z * piece, 8)
    total = sums[pl.ds(own, piece), :]
    for d in range(1, nz):
        copies[d - 1].wait_recv()
        total = total + zgot[d]
    zsums[pl.ds(own, piece), :] = total
    copies = []
    for d in range(1, nz):
        copies.append(begin(rcopy(zsums.at[pl.ds(own, piece)], zsums.at[pl.ds(own, piece)], zag_send.at[d], zag_recv.at[d], zdev[d])))
    for copy in copies:
        copy.wait_recv()

    for s in range(2):
        whole[pl.ds(pl.multiple_of(mine + offs[s], 8), size), :] = zsums[s * size : (s + 1) * size, :]
    for k in reversed(range(4)):
        size, offs = trail[k]
        copies = []
        for s in range(2):
            here = whole.at[pl.ds(pl.multiple_of(mine + offs[s], 8), size)]
            copies.append(begin(rcopy(here, here, ag_send.at[s, k], ag_recv.at[s, k], (steps[s][k][0], tensor))))
        if k == 2:
            poll(3)
        accumulate((nz - 3, 3, nz - 2, 2)[k])
        for copy in copies:
            copy.wait_recv()
    swap = begin(rcopy(whole.at[pl.ds(mine, rows)], whole.at[pl.ds(mine, rows)], core_send.at[1], core_recv.at[1], other))
    poll(4)
    accumulate(4)
    swap.wait_recv()

    wlen = mixed.shape[0] // 2
    woffs = dp_offsets(dp, core, wlen)

    def mixed_copy(k, s):
        size = wlen >> (k + 1)
        partner, bit = steps[s][k]
        keep = s * wlen + woffs[s] // size * size
        give = keep + (1 - 2 * bit) * size
        slot = mixed_got.at[s, pl.ds(wlen - 2 * size, size)]
        return rcopy(mixed.at[pl.ds(pl.multiple_of(give, 8), size)], slot, w_send.at[s, k], w_recv.at[s, k], (partner, tensor)), keep, size

    def mixed_add(k):
        for s in range(2):
            copy, keep, size = mixed_copy(k, s)
            copy.wait_recv()
            rows = pl.ds(pl.multiple_of(keep, 8), size)
            mixed[rows, :] = mixed[rows, :] + mixed_got[s, wlen - 2 * size : wlen - size, :]

    def mixed_send(k):
        for s in range(2):
            mixed_copy(k, s)[0].start()

    mixed_send(0)

    at = 0
    for i in range(nblk):
        for j in range(nblk):
            if j < i:
                inv_ref[i * NB : (i + 1) * NB, j * NB : (j + 1) * NB] = jnp.zeros((NB, NB), F32)
            else:
                inv_ref[i * NB : (i + 1) * NB, j * NB : (j + 1) * NB] = whole[at : at + NB, :]
                at += NB

    def between(k):
        for phase in range(3):
            @pl.when(k == phase + 2)
            def _():
                mixed_add(phase)
                mixed_send(phase + 1)

    chol_inv(inv_ref, block, between)

    mixed_add(3)
    size = wlen >> 4
    for s in range(2):
        mixed_ref[s * size : (s + 1) * size, :] = mixed[pl.ds(pl.multiple_of(s * wlen + woffs[s], 8), size), :]
    for k in range(4):
        for s in range(2):
            mixed_copy(k, s)[0].wait_send()
    for copy in pending:
        copy.wait_send()


def factor(projected, buffer):
    prows, n = projected.shape
    depth = buffer.shape[1]
    nblk = n // NB
    packed = nblk * (nblk + 1) // 2 * NB
    nz = lax.axis_size("tensor") // 2
    ndp = lax.axis_size("dp")
    rows = packed // 2
    last = rows // 2 // 16
    piece = -(-2 * last // (8 * nz)) * 8
    dma = pltpu.SemaphoreType.DMA
    vmem = pl.BlockSpec(memory_space=pltpu.VMEM)
    return pl.pallas_call(
        factor_kernel,
        out_shape=[
            jax.ShapeDtypeStruct((n, n), F32),
            jax.ShapeDtypeStruct((depth // ndp, n), F32),
            jax.ShapeDtypeStruct((prows * 2 * nz, n), F32),
        ],
        in_specs=[vmem] * 2,
        out_specs=[vmem] * 3,
        scratch_shapes=[
            pltpu.VMEM((packed, NB), F32),
            pltpu.VMEM((rows, NB), F32),
            pltpu.VMEM((2, rows // 2, NB), F32),
            pltpu.VMEM((piece * nz, NB), F32),
            pltpu.VMEM((nz, piece, NB), F32),
            pltpu.VMEM((piece * nz, NB), F32),
            pltpu.VMEM((packed, NB), F32),
            pltpu.VMEM((NB, NB), F32),
            pltpu.VMEM((depth, n), F32),
            pltpu.VMEM((2, depth // 2, n), F32),
            dma((2,)), dma((2,)), dma((2, 4)), dma((2, 4)), dma((nz,)), dma((nz,)),
            dma((2, 4)), dma((2, 4)), dma((nz,)), dma((nz,)),
            dma((nz // 2,)), dma((nz // 2,)), dma((nz // 2,)), dma((nz // 2,)), dma((nz,)), dma((nz,)),
            dma((2, 4)), dma((2, 4)),
        ],
        compiler_params=pltpu.CompilerParams(
            vmem_limit_bytes=56 << 20, collective_id=1, has_side_effects=True
        ),
        cost_estimate=pl.CostEstimate(flops=60_000_000_000, bytes_accessed=24 << 20, transcendentals=0),
        name="factor",
    )(projected, buffer)


def dp_offsets(dp, core, length):
    def bits(v):
        gray, high = lax.rem(v + v // 2, 2), v // 2
        other = 1 - core
        return [other * gray + core * high, other * high + core * gray]

    xs, ys = bits(lax.rem(dp, 4)), bits(dp // 4)
    out = []
    for order in (xs + ys, ys + xs):
        at, size = 0, length
        for bit in order:
            size //= 2
            at = at + bit * size
        out.append(at)
    return out


def finish_kernel(mixed_ref, inv_ref, proj_ref, ortho_ref, trans_ref, basis_ref, inv_hi, inv_lo, stacked, whole, sq, sq_t, sq_d, sq_sum, ag_send, ag_recv, t_send, t_recv, d_send, d_recv):
    dp, tensor = lax.axis_index("dp"), lax.axis_index("tensor")
    ndp, ntensor = lax.axis_size("dp"), lax.axis_size("tensor")
    core = lax.rem(tensor, 2)
    steps = dp_steps(core)
    tdev = [(dp, lax.rem(tensor + d, ntensor)) for d in range(ntensor)]
    ddev = [(lax.rem(dp + d, ndp), tensor) for d in range(ndp)]
    enter(tdev[1:] + ddev[1:])

    n = inv_ref.shape[0]
    for k in range(0, n, 256):
        wide = inv_ref[k : k + 256, :]
        high = wide.astype(BF16)
        inv_hi[k : k + 256, :] = high
        inv_lo[k : k + 256, :] = (wide - high.astype(F32)).astype(BF16)
    share = mixed_ref.shape[0]
    high = mixed_ref[...].astype(BF16)
    stacked[0:share, :] = high
    stacked[share:, :] = (mixed_ref[...] - high.astype(F32)).astype(BF16)
    length = whole.shape[0] // 2
    offs = dp_offsets(dp, core, length)
    spots = [pl.multiple_of(s * length + offs[s], 16) for s in range(2)]
    for k in range(0, n, 256):
        both = mm_nt(stacked[...], inv_hi[k : k + 256, :])
        part = both[0:share, :] + both[share:, :] + mm_nt(stacked[0:share, :], inv_lo[k : k + 256, :])
        squares = jnp.sum(part * part, axis=0, keepdims=True)
        for j in range(0, 256, NB):
            sq[(k + j) // NB : (k + j) // NB + 1, :] = squares[:, j : j + NB]
        part = part.astype(BF16)
        for s in range(2):
            whole[pl.ds(spots[s], share // 2), k : k + 256] = part[s * share // 2 : (s + 1) * share // 2, :]

    pending = []

    def gather_step(k):
        size = length >> (k + 1)
        copies = []
        for s in range(2):
            start = s * length + offs[s] // size * size
            region = whole.at[pl.ds(pl.multiple_of(start, 16), size)]
            copy = rcopy(region, region, ag_send.at[s, k], ag_recv.at[s, k], (steps[s][k][0], tensor))
            copy.start()
            copies.append(copy)
        pending.extend(copies)
        return copies

    def spread(source, slots, send, recv, devices):
        copies = []
        for d in range(1, len(devices)):
            copy = rcopy(source, slots.at[d], send.at[d], recv.at[d], devices[d])
            copy.start()
            copies.append(copy)
        pending.extend(copies)
        return copies

    def total(source, slots, copies):
        out = source[...]
        for d in range(1, slots.shape[0]):
            copies[d - 1].wait_recv()
            out = out + slots[d]
        return out

    def ortho_part(i):
        rows = proj_ref.shape[0] // 4
        rows0 = i * rows
        wide = proj_ref[rows0 : rows0 + rows, :]
        high = wide.astype(BF16)
        low = (wide - high.astype(F32)).astype(BF16)
        for k in range(0, n, 256):
            e = k + 256
            hi, lo = inv_hi[k:e, 0:e], inv_lo[k:e, 0:e]
            value = mm_nt(high[:, 0:e], hi) + (mm_nt(low[:, 0:e], hi) + mm_nt(high[:, 0:e], lo))
            ortho_ref[rows0 : rows0 + rows, k:e] = value.astype(BF16)

    across = spread(sq, sq_t, t_send, t_recv, tdev)
    copies = gather_step(3)
    ortho_part(0)
    sq_sum[...] = total(sq, sq_t, across)
    down = spread(sq_sum, sq_d, d_send, d_recv, ddev)
    for i, k in enumerate((2, 1, 0)):
        for copy in copies:
            copy.wait_recv()
        copies = gather_step(k)
        ortho_part(i + 1)
    scale = lax.rsqrt(total(sq_sum, sq_d, down) + NORM_EPS)
    for copy in copies:
        copy.wait_recv()
    for rows0 in range(0, whole.shape[0], NB):
        block = whole[rows0 : rows0 + NB, :]
        trans_ref[rows0 : rows0 + NB, :] = block
        for j in range(n // NB):
            basis_ref[rows0 : rows0 + NB, j * NB : (j + 1) * NB] = (
                block[:, j * NB : (j + 1) * NB].astype(F32) * scale[j : j + 1, :]
            ).astype(BF16)
    for copy in pending:
        copy.wait_send()


def finish(mixed, inverse, proj_all):
    share, n = mixed.shape
    rows = proj_all.shape[0]
    ndp, ntensor = lax.axis_size("dp"), lax.axis_size("tensor")
    dma = pltpu.SemaphoreType.DMA
    vmem = pl.BlockSpec(memory_space=pltpu.VMEM)
    return pl.pallas_call(
        finish_kernel,
        out_shape=[
            jax.ShapeDtypeStruct((rows, n), BF16),
            jax.ShapeDtypeStruct((share * ndp, n), BF16),
            jax.ShapeDtypeStruct((share * ndp, n), BF16),
        ],
        in_specs=[vmem] * 3,
        out_specs=[vmem] * 3,
        scratch_shapes=[
            pltpu.VMEM((n, n), BF16), pltpu.VMEM((n, n), BF16),
            pltpu.VMEM((2 * share, n), BF16), pltpu.VMEM((share * ndp, n), BF16),
            pltpu.VMEM((n // NB, NB), F32), pltpu.VMEM((ntensor, n // NB, NB), F32),
            pltpu.VMEM((ndp, n // NB, NB), F32), pltpu.VMEM((n // NB, NB), F32),
            dma((2, 4)), dma((2, 4)), dma((ntensor,)), dma((ntensor,)), dma((ndp,)), dma((ndp,)),
        ],
        compiler_params=pltpu.CompilerParams(
            vmem_limit_bytes=48 << 20, collective_id=2, has_side_effects=True
        ),
        cost_estimate=pl.CostEstimate(flops=20_000_000_000, bytes_accessed=16 << 20, transcendentals=0),
        name="finish",
    )(mixed, inverse, proj_all)


def project_kernel(buf_ref, share_ref, out_ref, basis, natural, part, swapped, acc, ring, ag_send, ag_recv, sw_send, sw_recv, ring_send, ring_recv):
    dp, tensor = lax.axis_index("dp"), lax.axis_index("tensor")
    ndp, nz = lax.axis_size("dp"), lax.axis_size("tensor") // 2
    core, z = lax.rem(tensor, 2), tensor // 2
    other = (dp, tensor + 1 - 2 * core)
    after = (dp, lax.rem(z + 1 - 2 * core + nz, nz) * 2 + core)
    before = (dp, lax.rem(z - 1 + 2 * core + nz, nz) * 2 + core)
    steps = dp_steps(core)
    enter([(partner, tensor) for partner, _ in steps[0]] + [other, after, before])
    pending = []

    share = share_ref.shape[0]
    length = basis.shape[0] // 2
    offs = dp_offsets(dp, core, length)
    half = share // 2
    for s in range(2):
        basis[pl.ds(pl.multiple_of(s * length + offs[s], 16), half), :] = share_ref[s * half : (s + 1) * half, :]
    for k in reversed(range(4)):
        size = length >> (k + 1)
        copies = []
        for s in range(2):
            region = basis.at[pl.ds(pl.multiple_of(s * length + offs[s] // size * size, 16), size)]
            copy = rcopy(region, region, ag_send.at[s, k], ag_recv.at[s, k], (steps[s][k][0], tensor))
            copy.start()
            copies.append(copy)
        for copy in copies:
            copy.wait_recv()
        pending += copies
    for d in range(ndp):
        there = dp_offsets(jnp.int32(d), core, length)
        for s in range(2):
            rows0 = d * share + s * half
            natural[rows0 : rows0 + half, :] = basis[pl.ds(pl.multiple_of(s * length + there[s], 16), half), :]

    chunk = buf_ref.shape[0] // nz
    rows = chunk // 2
    mine = pl.multiple_of(core * rows, 8)
    theirs = pl.multiple_of((1 - core) * rows, 8)

    def compute(r):
        rows0 = pl.multiple_of(lax.rem(z + r, nz) * chunk, 16)
        for k in range(0, natural.shape[0], 512):
            part[r, :, k : k + 512] = mm_nt(buf_ref[pl.ds(rows0, chunk), :], natural[k : k + 512, :])
        copy = rcopy(part.at[r, pl.ds(theirs, rows)], swapped.at[r], sw_send.at[r], sw_recv.at[r], other)
        copy.start()
        pending.append(copy)

    columns = out_ref.shape[1] // 2

    def term(r, h):
        return part[r, pl.ds(mine, rows), h * columns : (h + 1) * columns] + swapped[r, :, h * columns : (h + 1) * columns]

    def swap_wait(r):
        rcopy(part.at[r, pl.ds(theirs, rows)], swapped.at[r], sw_send.at[r], sw_recv.at[r], other).wait_recv()

    last = [None, None]

    def ring_step(s):
        r = core * (1 + s) + (1 - core) * (nz - 1 - s)
        swap_wait(r)
        for h in range(2):
            value = term(r, h)
            if s > 0:
                last[h].wait_recv()
                value = value + ring[s - 1, h]
            acc[s, h] = value
            last[h] = rcopy(acc.at[s, h], ring.at[s, h], ring_send.at[s, h], ring_recv.at[s, h], after)
            last[h].start()
            pending.append(last[h])

    order = []
    for r in range(1, nz // 2):
        order += [r, nz - r]
    order += [nz // 2, 0]
    done = 0
    for i in range(0, nz, 2):
        compute(order[i])
        compute(order[i + 1])
        if i >= 2:
            ring_step(done)
            done += 1
    for s in range(done, nz - 1):
        ring_step(s)
    swap_wait(0)
    for h in range(2):
        value = term(0, h)
        last[h].wait_recv()
        out_ref[:, h * columns : (h + 1) * columns] = value + ring[nz - 2, h]
    for copy in pending:
        copy.wait_send()


def project(buffer, share):
    nz = lax.axis_size("tensor") // 2
    n = share.shape[0] * lax.axis_size("dp")
    depth = share.shape[1]
    rows = buffer.shape[0] // nz // 2
    dma = pltpu.SemaphoreType.DMA
    vmem = pl.BlockSpec(memory_space=pltpu.VMEM)
    return pl.pallas_call(
        project_kernel,
        out_shape=jax.ShapeDtypeStruct((rows, n), F32),
        in_specs=[vmem] * 2,
        out_specs=vmem,
        scratch_shapes=[
            pltpu.VMEM((n, depth), BF16), pltpu.VMEM((n, depth), BF16),
            pltpu.VMEM((nz, 2 * rows, n), F32), pltpu.VMEM((nz, rows, n), F32),
            pltpu.VMEM((nz - 1, 2, rows, n // 2), F32), pltpu.VMEM((nz - 1, 2, rows, n // 2), F32),
            dma((2, 4)), dma((2, 4)), dma((nz,)), dma((nz,)), dma((nz - 1, 2)), dma((nz - 1, 2)),
        ],
        compiler_params=pltpu.CompilerParams(
            vmem_limit_bytes=48 << 20, collective_id=3, has_side_effects=True
        ),
        cost_estimate=pl.CostEstimate(flops=20_000_000_000, bytes_accessed=16 << 20, transcendentals=0),
        name="project",
    )(buffer, share)


def body(buffer, old_basis):
    groups = lax.axis_size("tensor")
    share = old_basis.shape[1]
    rank = share * lax.axis_size("dp")
    projected = project(buffer, old_basis.T)
    inverse, mixed, proj_all = factor(projected, buffer)
    ortho_all, trans_all, basis_all = finish(mixed, inverse, proj_all)
    new_basis = lax.dynamic_slice_in_dim(basis_all, lax.axis_index("dp") * share, share, axis=1)
    feedback = mm_nt(ortho_all, trans_all)
    new_buffer = (buffer.astype(F32) - FEEDBACK_SHARE * feedback).astype(BF16)
    scale_up = math.sqrt(
        buffer.shape[0] * lax.axis_size("dp") * buffer.shape[1] * groups / rank
    )
    product = mm_nt(ortho_all, basis_all)
    weight_update = (-scale_up * product).astype(BF16)
    return (new_buffer, weight_update, new_basis)


def solution(mesh):
    in_specs = (P("dp", "tensor"), P("tensor", "dp"))
    out_specs = (P("dp", "tensor"), P("dp", "tensor"), P("tensor", "dp"))
    return jax.shard_map(body, mesh=mesh, in_specs=in_specs, out_specs=out_specs, check_vma=False)
```

```python
import math

import jax
import jax.numpy as jnp
from jax import lax
from jax.experimental import pallas as pl
from jax.experimental.pallas import tpu as pltpu
from jax.sharding import PartitionSpec as P

NORM_EPS = 1e-06
FEEDBACK_SHARE = 0.05
HI = lax.Precision.HIGHEST
F32 = jnp.float32
BF16 = jnp.bfloat16
NB = 128
MP = 32


def mm_tn(a, b, precision=None):
    return lax.dot_general(
        a, b, (((0,), (0,)), ((), ())), precision=precision, preferred_element_type=F32
    )


def mm_nn(a, b, precision=None):
    return lax.dot_general(
        a, b, (((1,), (0,)), ((), ())), precision=precision, preferred_element_type=F32
    )


def mm_nt(a, b, precision=None):
    return lax.dot_general(
        a, b, (((1,), (1,)), ((), ())), precision=precision, preferred_element_type=F32
    )


def three(x):
    h = x.astype(BF16)
    rest = x - h.astype(F32)
    m = rest.astype(BF16)
    return h, m, (rest - m.astype(F32)).astype(BF16)


def eliminate_rows(rows, r0):
    lane = lax.broadcasted_iota(jnp.int32, (8, NB), 1)
    row = lax.broadcasted_iota(jnp.int32, (8, NB), 0)
    groups = MP // 8
    parts = [rows[8 * g : 8 * g + 8, :] for g in range(groups)]
    cols = [
        [jnp.broadcast_to(parts[g][:, r0 + c : r0 + c + 1], (8, NB)) if g >= c // 8 else None for g in range(groups)]
        for c in range(MP)
    ]
    scales = [jnp.zeros((8, NB), F32) for _ in range(groups)]

    def spread(value, i):
        return jnp.broadcast_to(value[i : i + 1, :], (8, NB))

    for c in range(MP):
        own, at = c // 8, c % 8
        rs = lax.rsqrt(spread(cols[c][own], at))
        inv = rs * rs
        f = [None] * groups
        for g in range(own, groups):
            f[g] = cols[c][g] * inv
        f[own] = jnp.where(row > at, f[own], 0.0)
        for c2 in range(c + 1, MP):
            e = spread(cols[c][c2 // 8], c2 % 8)
            for g in range(c2 // 8, groups):
                cols[c2][g] = cols[c2][g] - f[g] * e
        pivot = jnp.where(lane == r0 + c, 1.0, spread(parts[own], at))
        for g in range(groups):
            if g < own:
                parts[g] = jnp.where(lane == r0 + c, 0.0, parts[g])
            else:
                kept = jnp.where(lane == r0 + c, 0.0, parts[g])
                if g == own:
                    kept = jnp.where(row == at, pivot, kept)
                parts[g] = kept - f[g] * pivot
        scales[own] = jnp.where(row == at, rs, scales[own])
    return jnp.concatenate([p * v for p, v in zip(parts, scales)], axis=0)


def eliminate_block(block):
    lane = lax.broadcasted_iota(jnp.int32, (NB, NB), 1)
    for r0 in range(0, NB, MP):
        rows = eliminate_rows(block[r0 : r0 + MP, :], r0)
        block[r0 : r0 + MP, :] = rows
        if r0 + MP < NB:
            h, m, l = three(rows)
            left = jnp.concatenate([h, h, m, h, l, m], axis=0)
            right = jnp.concatenate([h, m, h, l, h, m], axis=0)
            update = mm_tn(left, right)[r0 + MP :, :]
            below = lane[r0 + MP :, :]
            old = jnp.where((below >= r0) & (below < r0 + MP), 0.0, block[r0 + MP :, :])
            block[r0 + MP :, :] = old - update


def chol_inv(out_ref, block, left, right, between):
    n = out_ref.shape[0]
    nblk = n // NB
    lane = lax.broadcasted_iota(jnp.int32, (NB, NB), 1)
    row = lax.broadcasted_iota(jnp.int32, (NB, NB), 0)

    def step(k, _):
        between(k)
        k0 = pl.multiple_of(k * NB, NB)
        block[...] = out_ref[pl.ds(k0, NB), pl.ds(k0, NB)]
        eliminate_block(block)
        linv = jnp.where(lane <= row, block[...], 0.0)
        out_ref[pl.ds(k0, NB), :] = mm_nn(linv, out_ref[pl.ds(k0, NB), :], HI)
        out_ref[pl.ds(k0, NB), pl.ds(k0, NB)] = linv
        h, m, l = three(out_ref[pl.ds(k0, NB), :])
        for j, (a, b) in enumerate(zip((h, h, m, h, l, m), (h, m, h, l, h, m))):
            left[j * NB : (j + 1) * NB, :] = a
            right[j * NB : (j + 1) * NB, :] = b

        def below(i0, size):
            out_ref[pl.ds(i0, size), pl.ds(k0, NB)] = jnp.zeros((size, NB), F32)
            out_ref[pl.ds(i0, size), :] = out_ref[pl.ds(i0, size), :] - mm_tn(
                left[:, pl.ds(i0, size)], right[...]
            )

        @pl.when(lax.rem(k, 2) == 0)
        def _():
            below(pl.multiple_of(k0 + NB, NB), NB)

        def pair(i, _):
            below(pl.multiple_of(i * 2 * NB, 2 * NB), 2 * NB)
            return 0

        lax.fori_loop(k // 2 + 1, nblk // 2, pair, 0)
        return 0

    lax.fori_loop(0, nblk, step, 0)
    for k0 in range(0, n - NB, NB):
        out_ref[k0 : k0 + NB, k0 + NB :] = jnp.zeros((NB, n - k0 - NB), F32)


def rcopy(src, dst, send_sem, recv_sem, device):
    return pltpu.make_async_remote_copy(
        src_ref=src, dst_ref=dst, send_sem=send_sem, recv_sem=recv_sem,
        device_id=device, device_id_type=pl.DeviceIdType.MESH,
    )


def dp_steps(core):
    dp = lax.axis_index("dp")
    x, y = lax.rem(dp, 4), dp // 4

    def pairs(v):
        gray, high = lax.rem(v + v // 2, 2), v // 2
        near, far = v + 1 - 2 * lax.rem(v, 2), 3 - v
        other = 1 - core
        return (
            (other * near + core * far, other * gray + core * high),
            (other * far + core * near, other * high + core * gray),
        )

    xs = [(y * 4 + v, bit) for v, bit in pairs(x)]
    ys = [(v * 4 + x, bit) for v, bit in pairs(y)]
    return (xs + ys, ys + xs)


def enter(devices):
    barrier = pltpu.get_barrier_semaphore()
    for device in devices:
        pl.semaphore_signal(barrier, inc=1, device_id=device, device_id_type=pl.DeviceIdType.MESH)
    pl.semaphore_wait(barrier, len(devices))


def dp_offsets(dp, core, length):
    def bits(v):
        gray, high = lax.rem(v + v // 2, 2), v // 2
        other = 1 - core
        return [other * gray + core * high, other * high + core * gray]

    xs, ys = bits(lax.rem(dp, 4)), bits(dp // 4)
    out = []
    for order in (xs + ys, ys + xs):
        at, size = 0, length
        for bit in order:
            size //= 2
            at = at + bit * size
        out.append(at)
    return out


def factor_kernel(
    p_ref, buf_ref, ortho_ref, trans_ref, basis_ref, inv_ref, all_ref, left, right, inv_hi, inv_lo, stacked, part, half, got, sums, zgot, zsums, whole, block, mixed, mixed_got, sq, sq_t, sq_d, sq_sum, core_send, core_recv, dp_send, dp_recv, z_send, z_recv, ag_send, ag_recv, zag_send, zag_recv, plus_send, plus_recv, minus_send, minus_recv, pair_send, pair_recv, w_send, w_recv, tr_send, tr_recv, t_send, t_recv, d_send, d_recv,
):
    dp, tensor = lax.axis_index("dp"), lax.axis_index("tensor")
    core, z = lax.rem(tensor, 2), tensor // 2
    nz = lax.axis_size("tensor") // 2
    other = (dp, tensor + 1 - 2 * core)
    steps = dp_steps(core)
    ndp, ntensor = lax.axis_size("dp"), 2 * nz
    zdev = [(dp, lax.rem(z + d, nz) * 2 + core) for d in range(nz)]
    tdev = [(dp, lax.rem(tensor + d, ntensor)) for d in range(ntensor)]
    ddev = [(lax.rem(dp + d, ndp), tensor) for d in range(ndp)]
    enter(tdev[1:] + ddev[1:])
    pending = []

    prows, n = p_ref.shape

    def region(r, c):
        at = (lax.rem(z + r, nz) * 2 + c) * prows
        return all_ref.at[pl.ds(pl.multiple_of(at, 8), prows)]

    def begin(copy):
        copy.start()
        pending.append(copy)
        return copy

    def pass_on(j):
        plus = region(nz - j if j else 0, core)
        begin(rcopy(plus, plus, plus_send.at[j], plus_recv.at[j], zdev[1]))
        if j < nz // 2 - 1:
            minus = region(j, core)
            begin(rcopy(minus, minus, minus_send.at[j], minus_recv.at[j], zdev[nz - 1]))

    def across(r):
        here = region(r, core)
        begin(rcopy(here, here, pair_send.at[r], pair_recv.at[r], other))

    def poll(j):
        here = region(nz - j, core)
        rcopy(here, here, plus_send.at[j - 1], plus_recv.at[j - 1], zdev[1]).wait_recv()
        if j < nz // 2:
            here = region(j, core)
            rcopy(here, here, minus_send.at[j - 1], minus_recv.at[j - 1], zdev[nz - 1]).wait_recv()
            pass_on(j)
            across(j)
        across(nz - j)

    chunk = 2 * prows

    def accumulate(r):
        here = region(r, core)
        rcopy(here, here, pair_send.at[r], pair_recv.at[r], other).wait_recv()
        rows0 = pl.multiple_of(lax.rem(z + r, nz) * chunk, 16)
        wide = all_ref[pl.ds(rows0, chunk), :]
        high = wide.astype(BF16)
        low = (wide - high.astype(F32)).astype(BF16)

        def strip(i, _):
            i0 = pl.multiple_of(i * 256, 256)
            left = buf_ref[pl.ds(rows0, chunk), pl.ds(i0, 256)]
            for k in range(0, n, 256):
                value = mm_tn(left, high[:, k : k + 256]) + mm_tn(left, low[:, k : k + 256])
                if r:
                    value = value + mixed[pl.ds(i0, 256), k : k + 256]
                mixed[pl.ds(i0, 256), k : k + 256] = value
            return 0

        lax.fori_loop(0, mixed.shape[0] // 256, strip, 0)

    own_rows = pl.multiple_of(tensor * prows, 8)
    all_ref[pl.ds(own_rows, prows), :] = p_ref[...]
    pass_on(0)
    across(0)

    nblk = n // NB
    order = [[0, 1, nblk - 2, nblk - 1], list(range(2, nblk - 2))]
    spots = {}
    for i in order[0] + order[1]:
        for j in range(i, nblk):
            spots[i, j] = len(spots) * NB
    rows = len(spots) * NB // 2
    mine = pl.multiple_of(core * rows, 8)
    theirs = pl.multiple_of((1 - core) * rows, 8)
    deep = -(-prows // 16) * 16
    padded = jnp.concatenate([p_ref[...], jnp.zeros((deep - prows, n), F32)], axis=0)
    h, m, l = three(padded)
    for j, (a, b) in enumerate(zip((h, h, m, h, l, m), (h, m, h, l, h, m))):
        left[j * deep : (j + 1) * deep, :] = a
        right[j * deep : (j + 1) * deep, :] = b

    def gram_half(which):
        for i in order[which][::2]:
            i0 = i * NB
            prod = mm_tn(left[0 : 6 * deep, i0 : i0 + 2 * NB], right[0 : 6 * deep, i0:])
            for i2 in (i, i + 1):
                for j in range(i2, nblk):
                    at = spots[i2, j]
                    part[at : at + NB, :] = prod[(i2 - i) * NB : (i2 - i + 1) * NB, (j - i) * NB : (j - i + 1) * NB]

    for c in range(2):
        @pl.when(core == c)
        def _():
            gram_half(1 - c)

    swap = begin(rcopy(part.at[pl.ds(theirs, rows)], half, core_send.at[0, 0], core_recv.at[0, 0], other))
    for c in range(2):
        @pl.when(core == c)
        def _():
            gram_half(c)

    swap.wait_recv()
    half[...] = half[...] + part[pl.ds(mine, rows), :]

    length = rows // 2
    offs = [jnp.int32(0), jnp.int32(length)]
    trail = []
    size = length
    got_at = 0
    for k in range(4):
        size //= 2
        copies = []
        for s in range(2):
            partner, bit = steps[s][k]
            keep = pl.multiple_of(offs[s] + bit * size, 8)
            give = pl.multiple_of(offs[s] + (1 - bit) * size, 8)
            copies.append(begin(rcopy(half.at[pl.ds(give, size)], got.at[s, pl.ds(got_at, size)], dp_send.at[s, k], dp_recv.at[s, k], (partner, tensor))))
            offs[s] = keep
        if k == 0:
            accumulate(0)
        elif k >= 2:
            accumulate((1, nz - 1)[k - 2])
        for s in range(2):
            copies[s].wait_recv()
            half[pl.ds(offs[s], size), :] = half[pl.ds(offs[s], size), :] + got[s, pl.ds(got_at, size), :]
        if k == 0:
            poll(1)
        trail.append((size, list(offs)))
        got_at += size

    sums[0:size, :] = half[pl.ds(offs[0], size), :]
    sums[size : 2 * size, :] = half[pl.ds(offs[1], size), :]
    piece = sums.shape[0] // nz
    if sums.shape[0] > 2 * size:
        sums[2 * size :, :] = jnp.zeros((sums.shape[0] - 2 * size, NB), F32)
    copies = []
    for d in range(1, nz):
        zto = lax.rem(z + d, nz)
        copies.append(begin(rcopy(sums.at[pl.ds(pl.multiple_of(zto * piece, 8), piece)], zgot.at[d], z_send.at[d], z_recv.at[d], zdev[d])))
    poll(2)
    own = pl.multiple_of(z * piece, 8)
    total = sums[pl.ds(own, piece), :]
    for d in range(1, nz):
        copies[d - 1].wait_recv()
        total = total + zgot[d]
    zsums[pl.ds(own, piece), :] = total
    copies = []
    for d in range(1, nz):
        copies.append(begin(rcopy(zsums.at[pl.ds(own, piece)], zsums.at[pl.ds(own, piece)], zag_send.at[d], zag_recv.at[d], zdev[d])))
    for copy in copies:
        copy.wait_recv()

    def to_other(stage, s, start, count):
        here = whole.at[pl.ds(pl.multiple_of(mine + start, 8), count)]
        return begin(rcopy(here, here, core_send.at[s, stage], core_recv.at[s, stage], other))

    passed = []
    for s in range(2):
        whole[pl.ds(pl.multiple_of(mine + offs[s], 8), size), :] = zsums[s * size : (s + 1) * size, :]
        passed.append(to_other(1, s, offs[s], size))
    for k in reversed(range(4)):
        size, offs = trail[k]
        copies = []
        for s in range(2):
            here = whole.at[pl.ds(pl.multiple_of(mine + offs[s], 8), size)]
            copies.append(begin(rcopy(here, here, ag_send.at[s, k], ag_recv.at[s, k], (steps[s][k][0], tensor))))
        if k == 2:
            poll(3)
        accumulate((nz - 3, 3, nz - 2, 2)[k])
        for s in range(2):
            copies[s].wait_recv()
            passed.append(to_other(5 - k, s, offs[s] + (1 - 2 * steps[s][k][1]) * size, size))
    poll(4)
    accumulate(4)
    for copy in passed:
        copy.wait_recv()

    wlen = mixed.shape[0] // 2
    woffs = dp_offsets(dp, core, wlen)

    def mixed_copy(k, s):
        size = wlen >> (k + 1)
        partner, bit = steps[s][k]
        keep = s * wlen + woffs[s] // size * size
        give = keep + (1 - 2 * bit) * size
        slot = mixed_got.at[s, pl.ds(wlen - 2 * size, size)]
        return rcopy(mixed.at[pl.ds(pl.multiple_of(give, 8), size)], slot, w_send.at[s, k], w_recv.at[s, k], (partner, tensor)), keep, size

    def mixed_add(k):
        for s in range(2):
            copy, keep, size = mixed_copy(k, s)
            copy.wait_recv()
            rows = pl.ds(pl.multiple_of(keep, 8), size)
            mixed[rows, :] = mixed[rows, :] + mixed_got[s, wlen - 2 * size : wlen - size, :]

    def mixed_send(k):
        for s in range(2):
            mixed_copy(k, s)[0].start()

    mixed_send(0)

    for i in range(nblk):
        for j in range(nblk):
            if j < i:
                value = jnp.zeros((NB, NB), F32)
            else:
                value = whole[spots[i, j] : spots[i, j] + NB, :]
            inv_ref[i * NB : (i + 1) * NB, j * NB : (j + 1) * NB] = value

    def between(k):
        for phase in range(3):
            @pl.when(k == phase + 2)
            def _():
                mixed_add(phase)
                mixed_send(phase + 1)

    chol_inv(inv_ref, block, left, right, between)

    for k in range(0, n, 256):
        wide = inv_ref[k : k + 256, :]
        high = wide.astype(BF16)
        inv_hi[k : k + 256, :] = high
        inv_lo[k : k + 256, :] = (wide - high.astype(F32)).astype(BF16)
    mixed_add(3)
    piece = wlen >> 4
    share = 2 * piece
    rows_at = [pl.multiple_of(s * wlen + woffs[s], 16) for s in range(2)]
    for s in range(2):
        wide = mixed[pl.ds(rows_at[s], piece), :]
        high = wide.astype(BF16)
        stacked[s * piece : (s + 1) * piece, :] = high
        stacked[share + s * piece : share + (s + 1) * piece, :] = (wide - high.astype(F32)).astype(BF16)
    for k in range(0, n, 256):
        both = mm_nt(stacked[...], inv_hi[k : k + 256, :])
        trans = both[0:share, :] + both[share:, :] + mm_nt(stacked[0:share, :], inv_lo[k : k + 256, :])
        squares = jnp.sum(trans * trans, axis=0, keepdims=True)
        for j in range(0, 256, NB):
            sq[(k + j) // NB : (k + j) // NB + 1, :] = squares[:, j : j + NB]
        half_part = trans.astype(BF16)
        for s in range(2):
            trans_ref[pl.ds(rows_at[s], piece), k : k + 256] = half_part[s * piece : (s + 1) * piece, :]

    def gather_step(k):
        size = wlen >> (k + 1)
        copies = []
        for s in range(2):
            start = s * wlen + woffs[s] // size * size
            here = trans_ref.at[pl.ds(pl.multiple_of(start, 16), size)]
            copies.append(begin(rcopy(here, here, tr_send.at[s, k], tr_recv.at[s, k], (steps[s][k][0], tensor))))
        return copies

    def spread(source, slots, send, recv, devices):
        copies = []
        for d in range(1, len(devices)):
            copies.append(begin(rcopy(source, slots.at[d], send.at[d], recv.at[d], devices[d])))
        return copies

    def sum_of(source, slots, copies):
        out = source[...]
        for d in range(1, slots.shape[0]):
            copies[d - 1].wait_recv()
            out = out + slots[d]
        return out

    def ortho_part(i):
        count = all_ref.shape[0] // 4
        rows0 = i * count
        wide = all_ref[rows0 : rows0 + count, :]
        high = wide.astype(BF16)
        low = (wide - high.astype(F32)).astype(BF16)
        for k in range(0, n, 256):
            e = k + 256
            hi, lo = inv_hi[k:e, 0:e], inv_lo[k:e, 0:e]
            value = mm_nt(high[:, 0:e], hi) + (mm_nt(low[:, 0:e], hi) + mm_nt(high[:, 0:e], lo))
            ortho_ref[rows0 : rows0 + count, k:e] = value.astype(BF16)

    beside = spread(sq, sq_t, t_send, t_recv, tdev)
    copies = gather_step(3)
    ortho_part(0)
    sq_sum[...] = sum_of(sq, sq_t, beside)
    down = spread(sq_sum, sq_d, d_send, d_recv, ddev)
    for i, k in enumerate((2, 1, 0)):
        for copy in copies:
            copy.wait_recv()
        copies = gather_step(k)
        ortho_part(i + 1)
    scale = lax.rsqrt(sum_of(sq_sum, sq_d, down) + NORM_EPS)
    for copy in copies:
        copy.wait_recv()
    for rows0 in range(0, trans_ref.shape[0], NB):
        for j in range(n // NB):
            value = trans_ref[rows0 : rows0 + NB, j * NB : (j + 1) * NB].astype(F32)
            basis_ref[rows0 : rows0 + NB, j * NB : (j + 1) * NB] = (value * scale[j : j + 1, :]).astype(BF16)
    for k in range(4):
        for s in range(2):
            mixed_copy(k, s)[0].wait_send()
    for copy in pending:
        copy.wait_send()


def factor(projected, buffer):
    prows, n = projected.shape
    depth = buffer.shape[1]
    nblk = n // NB
    packed = nblk * (nblk + 1) // 2 * NB
    ntensor, ndp = lax.axis_size("tensor"), lax.axis_size("dp")
    nz = ntensor // 2
    rows = packed // 2
    last = rows // 2 // 16
    piece = -(-2 * last // (8 * nz)) * 8
    dma = pltpu.SemaphoreType.DMA
    vmem = pl.BlockSpec(memory_space=pltpu.VMEM)

    def f32(*shape):
        return pltpu.VMEM(shape, F32)

    def bf16(*shape):
        return pltpu.VMEM(shape, BF16)

    return pl.pallas_call(
        factor_kernel,
        out_shape=[
            jax.ShapeDtypeStruct((prows * ntensor, n), BF16),
            jax.ShapeDtypeStruct((depth, n), BF16),
            jax.ShapeDtypeStruct((depth, n), BF16),
        ],
        in_specs=[vmem] * 2,
        out_specs=[vmem] * 3,
        scratch_shapes=[
            f32(n, n), f32(prows * ntensor, n), bf16(6 * NB, n), bf16(6 * NB, n),
            bf16(n, n), bf16(n, n), bf16(2 * depth // ndp, n),
            f32(packed, NB), f32(rows, NB), f32(2, rows // 2, NB),
            f32(piece * nz, NB), f32(nz, piece, NB), f32(piece * nz, NB), f32(packed, NB),
            f32(NB, NB), f32(depth, n), f32(2, depth // 2, n),
            f32(nblk, NB), f32(ntensor, nblk, NB), f32(ndp, nblk, NB), f32(nblk, NB),
            dma((2, 6)), dma((2, 6)), dma((2, 4)), dma((2, 4)), dma((nz,)), dma((nz,)),
            dma((2, 4)), dma((2, 4)), dma((nz,)), dma((nz,)),
            dma((nz // 2,)), dma((nz // 2,)), dma((nz // 2,)), dma((nz // 2,)), dma((nz,)), dma((nz,)),
            dma((2, 4)), dma((2, 4)), dma((2, 4)), dma((2, 4)),
            dma((ntensor,)), dma((ntensor,)), dma((ndp,)), dma((ndp,)),
        ],
        compiler_params=pltpu.CompilerParams(
            vmem_limit_bytes=58 << 20, collective_id=1, has_side_effects=True
        ),
        cost_estimate=pl.CostEstimate(flops=60_000_000_000, bytes_accessed=24 << 20, transcendentals=0),
        name="factor",
    )(projected, buffer)


def project_kernel(buf_ref, share_ref, out_ref, basis, natural, part, swapped, acc, ring, ag_send, ag_recv, sw_send, sw_recv, ring_send, ring_recv):
    dp, tensor = lax.axis_index("dp"), lax.axis_index("tensor")
    ndp, nz = lax.axis_size("dp"), lax.axis_size("tensor") // 2
    core, z = lax.rem(tensor, 2), tensor // 2
    other = (dp, tensor + 1 - 2 * core)
    after = (dp, lax.rem(z + 1 - 2 * core + nz, nz) * 2 + core)
    before = (dp, lax.rem(z - 1 + 2 * core + nz, nz) * 2 + core)
    steps = dp_steps(core)
    enter([(partner, tensor) for partner, _ in steps[0]] + [other, after, before])
    pending = []

    share = share_ref.shape[0]
    length = basis.shape[0] // 2
    offs = dp_offsets(dp, core, length)
    half = share // 2
    for s in range(2):
        basis[pl.ds(pl.multiple_of(s * length + offs[s], 16), half), :] = share_ref[s * half : (s + 1) * half, :]
    for k in reversed(range(4)):
        size = length >> (k + 1)
        copies = []
        for s in range(2):
            region = basis.at[pl.ds(pl.multiple_of(s * length + offs[s] // size * size, 16), size)]
            copy = rcopy(region, region, ag_send.at[s, k], ag_recv.at[s, k], (steps[s][k][0], tensor))
            copy.start()
            copies.append(copy)
        for copy in copies:
            copy.wait_recv()
        pending += copies
    for d in range(ndp):
        there = dp_offsets(jnp.int32(d), core, length)
        for s in range(2):
            rows0 = d * share + s * half
            natural[rows0 : rows0 + half, :] = basis[pl.ds(pl.multiple_of(s * length + there[s], 16), half), :]

    chunk = buf_ref.shape[0] // nz
    rows = chunk // 2
    mine = pl.multiple_of(core * rows, 8)
    theirs = pl.multiple_of((1 - core) * rows, 8)

    def compute(r):
        rows0 = pl.multiple_of(lax.rem(z + r, nz) * chunk, 16)
        for k in range(0, natural.shape[0], 512):
            part[r, :, k : k + 512] = mm_nt(buf_ref[pl.ds(rows0, chunk), :], natural[k : k + 512, :])
        copy = rcopy(part.at[r, pl.ds(theirs, rows)], swapped.at[r], sw_send.at[r], sw_recv.at[r], other)
        copy.start()
        pending.append(copy)

    columns = out_ref.shape[1] // 2

    def term(r, h):
        return part[r, pl.ds(mine, rows), h * columns : (h + 1) * columns] + swapped[r, :, h * columns : (h + 1) * columns]

    def swap_wait(r):
        rcopy(part.at[r, pl.ds(theirs, rows)], swapped.at[r], sw_send.at[r], sw_recv.at[r], other).wait_recv()

    last = [None, None]

    def ring_step(s):
        r = core * (1 + s) + (1 - core) * (nz - 1 - s)
        swap_wait(r)
        for h in range(2):
            value = term(r, h)
            if s > 0:
                last[h].wait_recv()
                value = value + ring[s - 1, h]
            acc[s, h] = value
            last[h] = rcopy(acc.at[s, h], ring.at[s, h], ring_send.at[s, h], ring_recv.at[s, h], after)
            last[h].start()
            pending.append(last[h])

    order = []
    for r in range(1, nz // 2):
        order += [r, nz - r]
    order += [nz // 2, 0]
    done = 0
    for i in range(0, nz, 2):
        compute(order[i])
        compute(order[i + 1])
        if i >= 2:
            ring_step(done)
            done += 1
    for s in range(done, nz - 1):
        ring_step(s)
    swap_wait(0)
    for h in range(2):
        value = term(0, h)
        last[h].wait_recv()
        out_ref[:, h * columns : (h + 1) * columns] = value + ring[nz - 2, h]
    for copy in pending:
        copy.wait_send()


def project(buffer, share):
    nz = lax.axis_size("tensor") // 2
    n = share.shape[0] * lax.axis_size("dp")
    depth = share.shape[1]
    rows = buffer.shape[0] // nz // 2
    dma = pltpu.SemaphoreType.DMA
    vmem = pl.BlockSpec(memory_space=pltpu.VMEM)
    return pl.pallas_call(
        project_kernel,
        out_shape=jax.ShapeDtypeStruct((rows, n), F32),
        in_specs=[vmem] * 2,
        out_specs=vmem,
        scratch_shapes=[
            pltpu.VMEM((n, depth), BF16), pltpu.VMEM((n, depth), BF16),
            pltpu.VMEM((nz, 2 * rows, n), F32), pltpu.VMEM((nz, rows, n), F32),
            pltpu.VMEM((nz - 1, 2, rows, n // 2), F32), pltpu.VMEM((nz - 1, 2, rows, n // 2), F32),
            dma((2, 4)), dma((2, 4)), dma((nz,)), dma((nz,)), dma((nz - 1, 2)), dma((nz - 1, 2)),
        ],
        compiler_params=pltpu.CompilerParams(
            vmem_limit_bytes=48 << 20, collective_id=3, has_side_effects=True
        ),
        cost_estimate=pl.CostEstimate(flops=20_000_000_000, bytes_accessed=16 << 20, transcendentals=0),
        name="project",
    )(buffer, share)


def body(buffer, old_basis):
    groups = lax.axis_size("tensor")
    share = old_basis.shape[1]
    rank = share * lax.axis_size("dp")
    projected = project(buffer, old_basis.T)
    ortho_all, trans_all, basis_all = factor(projected, buffer)
    new_basis = lax.dynamic_slice_in_dim(basis_all, lax.axis_index("dp") * share, share, axis=1)
    feedback = mm_nt(ortho_all, trans_all)
    new_buffer = (buffer.astype(F32) - FEEDBACK_SHARE * feedback).astype(BF16)
    scale_up = math.sqrt(
        buffer.shape[0] * lax.axis_size("dp") * buffer.shape[1] * groups / rank
    )
    product = mm_nt(ortho_all, basis_all)
    weight_update = (-scale_up * product).astype(BF16)
    return (new_buffer, weight_update, new_basis)


def solution(mesh):
    in_specs = (P("dp", "tensor"), P("tensor", "dp"))
    out_specs = (P("dp", "tensor"), P("dp", "tensor"), P("tensor", "dp"))
    return jax.shard_map(body, mesh=mesh, in_specs=in_specs, out_specs=out_specs, check_vma=False)
```

```python
import functools
import math

import jax
import jax.numpy as jnp
from jax import lax
from jax.experimental import pallas as pl
from jax.experimental.pallas import tpu as pltpu
from jax.sharding import PartitionSpec as P

NORM_EPS = 1e-06
FEEDBACK_SHARE = 0.05
HI = lax.Precision.HIGHEST
F32 = jnp.float32
BF16 = jnp.bfloat16
NB = 128
MP = 32


def mm_tn(a, b, precision=None):
    return lax.dot_general(
        a, b, (((0,), (0,)), ((), ())), precision=precision, preferred_element_type=F32
    )


def mm_nn(a, b, precision=None):
    return lax.dot_general(
        a, b, (((1,), (0,)), ((), ())), precision=precision, preferred_element_type=F32
    )


def mm_nt(a, b, precision=None):
    return lax.dot_general(
        a, b, (((1,), (1,)), ((), ())), precision=precision, preferred_element_type=F32
    )


def three(x):
    h = x.astype(BF16)
    rest = x - h.astype(F32)
    m = rest.astype(BF16)
    return h, m, (rest - m.astype(F32)).astype(BF16)


def eliminate_rows(rows, r0):
    lane = lax.broadcasted_iota(jnp.int32, (8, NB), 1)
    row = lax.broadcasted_iota(jnp.int32, (8, NB), 0)
    groups = MP // 8
    parts = [rows[8 * g : 8 * g + 8, :] for g in range(groups)]
    cols = [
        [jnp.broadcast_to(parts[g][:, r0 + c : r0 + c + 1], (8, NB)) if g >= c // 8 else None for g in range(groups)]
        for c in range(MP)
    ]
    scales = [jnp.zeros((8, NB), F32) for _ in range(groups)]

    def spread(value, i):
        return jnp.broadcast_to(value[i : i + 1, :], (8, NB))

    for c in range(MP):
        own, at = c // 8, c % 8
        rs = lax.rsqrt(spread(cols[c][own], at))
        inv = rs * rs
        f = [None] * groups
        for g in range(own, groups):
            f[g] = cols[c][g] * inv
        f[own] = jnp.where(row > at, f[own], 0.0)
        for c2 in range(c + 1, MP):
            e = spread(cols[c][c2 // 8], c2 % 8)
            for g in range(c2 // 8, groups):
                cols[c2][g] = cols[c2][g] - f[g] * e
        pivot = jnp.where(lane == r0 + c, 1.0, spread(parts[own], at))
        for g in range(groups):
            if g < own:
                parts[g] = jnp.where(lane == r0 + c, 0.0, parts[g])
            else:
                kept = jnp.where(lane == r0 + c, 0.0, parts[g])
                if g == own:
                    kept = jnp.where(row == at, pivot, kept)
                parts[g] = kept - f[g] * pivot
        scales[own] = jnp.where(row == at, rs, scales[own])
    return jnp.concatenate([p * v for p, v in zip(parts, scales)], axis=0)


def eliminate_block(block):
    lane = lax.broadcasted_iota(jnp.int32, (NB, NB), 1)
    for r0 in range(0, NB, MP):
        rows = eliminate_rows(block[r0 : r0 + MP, :], r0)
        block[r0 : r0 + MP, :] = rows
        if r0 + MP < NB:
            h, m, l = three(rows)
            left = jnp.concatenate([h, h, m, h, l, m], axis=0)
            right = jnp.concatenate([h, m, h, l, h, m], axis=0)
            update = mm_tn(left, right)[r0 + MP :, :]
            below = lane[r0 + MP :, :]
            old = jnp.where((below >= r0) & (below < r0 + MP), 0.0, block[r0 + MP :, :])
            block[r0 + MP :, :] = old - update


def chol_inv(out_ref, block, left, right, between):
    n = out_ref.shape[0]
    nblk = n // NB
    lane = lax.broadcasted_iota(jnp.int32, (NB, NB), 1)
    row = lax.broadcasted_iota(jnp.int32, (NB, NB), 0)

    def step(k, _):
        between(k)
        k0 = pl.multiple_of(k * NB, NB)
        block[...] = out_ref[pl.ds(k0, NB), pl.ds(k0, NB)]
        eliminate_block(block)
        linv = jnp.where(lane <= row, block[...], 0.0)
        out_ref[pl.ds(k0, NB), :] = mm_nn(linv, out_ref[pl.ds(k0, NB), :], HI)
        out_ref[pl.ds(k0, NB), pl.ds(k0, NB)] = linv
        h, m, l = three(out_ref[pl.ds(k0, NB), :])
        for j, (a, b) in enumerate(zip((h, h, m, h, l, m), (h, m, h, l, h, m))):
            left[j * NB : (j + 1) * NB, :] = a
            right[j * NB : (j + 1) * NB, :] = b

        def below(i0, size):
            out_ref[pl.ds(i0, size), pl.ds(k0, NB)] = jnp.zeros((size, NB), F32)
            out_ref[pl.ds(i0, size), :] = out_ref[pl.ds(i0, size), :] - mm_tn(
                left[:, pl.ds(i0, size)], right[...]
            )

        @pl.when(lax.rem(k, 2) == 0)
        def _():
            below(pl.multiple_of(k0 + NB, NB), NB)

        def pair(i, _):
            below(pl.multiple_of(i * 2 * NB, 2 * NB), 2 * NB)
            return 0

        lax.fori_loop(k // 2 + 1, nblk // 2, pair, 0)
        return 0

    lax.fori_loop(0, nblk, step, 0)
    for k0 in range(0, n - NB, NB):
        out_ref[k0 : k0 + NB, k0 + NB :] = jnp.zeros((NB, n - k0 - NB), F32)


def rcopy(src, dst, send_sem, recv_sem, device):
    return pltpu.make_async_remote_copy(
        src_ref=src, dst_ref=dst, send_sem=send_sem, recv_sem=recv_sem,
        device_id=device, device_id_type=pl.DeviceIdType.MESH,
    )


def dp_steps(core):
    dp = lax.axis_index("dp")
    x, y = lax.rem(dp, 4), dp // 4

    def pairs(v):
        gray, high = lax.rem(v + v // 2, 2), v // 2
        near, far = v + 1 - 2 * lax.rem(v, 2), 3 - v
        other = 1 - core
        return (
            (other * near + core * far, other * gray + core * high),
            (other * far + core * near, other * high + core * gray),
        )

    xs = [(y * 4 + v, bit) for v, bit in pairs(x)]
    ys = [(v * 4 + x, bit) for v, bit in pairs(y)]
    return (xs + ys, ys + xs)


def enter(devices):
    barrier = pltpu.get_barrier_semaphore()
    for device in devices:
        pl.semaphore_signal(barrier, inc=1, device_id=device, device_id_type=pl.DeviceIdType.MESH)
    pl.semaphore_wait(barrier, len(devices))


def dp_offsets(dp, core, length):
    def bits(v):
        gray, high = (v + v // 2) % 2, v // 2
        other = 1 - core
        return [other * gray + core * high, other * high + core * gray]

    xs, ys = bits(dp % 4), bits(dp // 4)
    out = []
    for order in (xs + ys, ys + xs):
        at, size = 0, length
        for bit in order:
            size //= 2
            at = at + bit * size
        out.append(at)
    return out


def factor_kernel(
    p_ref, buf_ref, ortho_ref, trans_ref, basis_ref, inv_ref, all_ref, left, right, inv_hi, inv_lo, stacked, part, half, got, sums, zgot, zsums, whole, block, mixed, mixed_got, sq, sq_t, sq_d, sq_sum, core_send, core_recv, dp_send, dp_recv, z_send, z_recv, ag_send, ag_recv, zag_send, zag_recv, plus_send, plus_recv, minus_send, minus_recv, pair_send, pair_recv, w_send, w_recv, tr_send, tr_recv, t_send, t_recv, d_send, d_recv,
):
    dp, tensor = lax.axis_index("dp"), lax.axis_index("tensor")
    core, z = lax.rem(tensor, 2), tensor // 2
    nz = lax.axis_size("tensor") // 2
    other = (dp, tensor + 1 - 2 * core)
    steps = dp_steps(core)
    ndp, ntensor = lax.axis_size("dp"), 2 * nz
    zdev = [(dp, lax.rem(z + d, nz) * 2 + core) for d in range(nz)]
    tdev = [(dp, lax.rem(tensor + d, ntensor)) for d in range(ntensor)]
    ddev = [(lax.rem(dp + d, ndp), tensor) for d in range(ndp)]
    enter(tdev[1:] + ddev[1:])
    pending = []

    prows, n = p_ref.shape

    places = [lax.rem(z + (1 - 2 * core) * r + nz, nz) for r in range(nz)]
    ahead, behind = [(dp, places[r] * 2 + core) for r in (1, nz - 1)]

    own_at = [pl.multiple_of((places[r] * 2 + core) * prows, 8) for r in range(nz)]

    def region(r):
        return all_ref.at[pl.ds(own_at[r], prows)]

    def begin(copy):
        copy.start()
        pending.append(copy)
        return copy

    def pass_on(j):
        plus = region(nz - j if j else 0)
        begin(rcopy(plus, plus, plus_send.at[j], plus_recv.at[j], ahead))
        if j < nz // 2 - 1:
            minus = region(j)
            begin(rcopy(minus, minus, minus_send.at[j], minus_recv.at[j], behind))

    def pair_copy(r):
        here = region(r)
        return rcopy(here, here, pair_send.at[r], pair_recv.at[r], other)

    def across(r):
        pair_copy(r).start()

    def poll(j):
        here = region(nz - j)
        rcopy(here, here, plus_send.at[j - 1], plus_recv.at[j - 1], ahead).wait_recv()
        if j < nz // 2:
            here = region(j)
            rcopy(here, here, minus_send.at[j - 1], minus_recv.at[j - 1], behind).wait_recv()
            pass_on(j)
            across(j)
        across(nz - j)

    chunk = 2 * prows
    chunk_at = [pl.multiple_of(places[r] * chunk, 16) for r in range(nz)]

    def accumulate(r):
        here = region(r)
        rcopy(here, here, pair_send.at[r], pair_recv.at[(nz - r) % nz], other).wait_recv()
        rows0 = chunk_at[r]
        wide = all_ref[pl.ds(rows0, chunk), :]
        high = wide.astype(BF16)
        low = (wide - high.astype(F32)).astype(BF16)

        for i0 in range(0, mixed.shape[0], 256):
            columns = buf_ref[pl.ds(rows0, chunk), i0 : i0 + 256]
            for k in range(0, n, 256):
                value = mm_tn(columns, high[:, k : k + 256]) + mm_tn(columns, low[:, k : k + 256])
                if r:
                    value = value + mixed[i0 : i0 + 256, k : k + 256]
                mixed[i0 : i0 + 256, k : k + 256] = value

    own_rows = pl.multiple_of(tensor * prows, 8)
    all_ref[pl.ds(own_rows, prows), :] = p_ref[...]
    pass_on(0)
    across(0)

    nblk = n // NB
    order = [[0, 1, nblk - 2, nblk - 1], list(range(2, nblk - 2))]
    spots = {}
    for i in order[0] + order[1]:
        for j in range(i, nblk):
            spots[i, j] = len(spots) * NB
    rows = len(spots) * NB // 2
    mine = pl.multiple_of(core * rows, 8)
    theirs = pl.multiple_of((1 - core) * rows, 8)
    deep = -(-prows // 16) * 16
    padded = jnp.concatenate([p_ref[...], jnp.zeros((deep - prows, n), F32)], axis=0)
    h, m, l = three(padded)
    for j, (a, b) in enumerate(zip((h, h, m, h, l, m), (h, m, h, l, h, m))):
        left[j * deep : (j + 1) * deep, :] = a
        right[j * deep : (j + 1) * deep, :] = b

    def gram_half(which):
        for i in order[which][::2]:
            i0 = i * NB
            prod = mm_tn(left[0 : 6 * deep, i0 : i0 + 2 * NB], right[0 : 6 * deep, i0:])
            for i2 in (i, i + 1):
                for j in range(i2, nblk):
                    at = spots[i2, j]
                    part[at : at + NB, :] = prod[(i2 - i) * NB : (i2 - i + 1) * NB, (j - i) * NB : (j - i + 1) * NB]

    for c in range(2):
        @pl.when(core == c)
        def _():
            gram_half(1 - c)

    swap = begin(rcopy(part.at[pl.ds(theirs, rows)], half, core_send.at[0, 0], core_recv.at[0, 0], other))
    for c in range(2):
        @pl.when(core == c)
        def _():
            gram_half(c)

    swap.wait_recv()
    half[...] = half[...] + part[pl.ds(mine, rows), :]

    length = rows // 2
    offs = [0, length]
    trail = []
    size = length
    got_at = 0
    for k in range(4):
        size //= 2
        copies = []
        for s in range(2):
            partner, bit = steps[s][k]
            keep = pl.multiple_of(offs[s] + bit * size, 8)
            give = pl.multiple_of(offs[s] + (1 - bit) * size, 8)
            copies.append(begin(rcopy(half.at[pl.ds(give, size)], got.at[s, pl.ds(got_at, size)], dp_send.at[s, k], dp_recv.at[s, k], (partner, tensor))))
            offs[s] = keep
        if k == 0:
            accumulate(0)
        for s in range(2):
            copies[s].wait_recv()
            half[pl.ds(offs[s], size), :] = half[pl.ds(offs[s], size), :] + got[s, pl.ds(got_at, size), :]
        if k == 0:
            poll(1)
        trail.append((size, list(offs)))
        got_at += size

    sums[0:size, :] = half[pl.ds(offs[0], size), :]
    sums[size : 2 * size, :] = half[pl.ds(offs[1], size), :]
    piece = sums.shape[0] // nz
    if sums.shape[0] > 2 * size:
        sums[2 * size :, :] = jnp.zeros((sums.shape[0] - 2 * size, NB), F32)
    copies = []
    for d in range(1, nz):
        zto = lax.rem(z + d, nz)
        copies.append(begin(rcopy(sums.at[pl.ds(pl.multiple_of(zto * piece, 8), piece)], zgot.at[d], z_send.at[d], z_recv.at[d], zdev[d])))
    own = pl.multiple_of(z * piece, 8)
    total = sums[pl.ds(own, piece), :]
    for d in range(1, nz):
        copies[d - 1].wait_recv()
        total = total + zgot[d]
    zsums[pl.ds(own, piece), :] = total
    copies = []
    for d in range(1, nz):
        copies.append(begin(rcopy(zsums.at[pl.ds(own, piece)], zsums.at[pl.ds(own, piece)], zag_send.at[d], zag_recv.at[d], zdev[d])))
    for copy in copies:
        copy.wait_recv()
    poll(2)

    def to_other(stage, s, start, count):
        here = whole.at[pl.ds(pl.multiple_of(mine + start, 8), count)]
        return begin(rcopy(here, here, core_send.at[s, stage], core_recv.at[s, stage], other))

    passed = []
    for s in range(2):
        whole[pl.ds(pl.multiple_of(mine + offs[s], 8), size), :] = zsums[s * size : (s + 1) * size, :]
        passed.append(to_other(1, s, offs[s], size))
    for k in reversed(range(4)):
        size, offs = trail[k]
        copies = []
        for s in range(2):
            here = whole.at[pl.ds(pl.multiple_of(mine + offs[s], 8), size)]
            copies.append(begin(rcopy(here, here, ag_send.at[s, k], ag_recv.at[s, k], (steps[s][k][0], tensor))))
        if k == 3:
            accumulate(1)
        elif k == 2:
            accumulate(nz - 1)
        elif k == 0:
            poll(3)
            accumulate(2)
            accumulate(nz - 2)
        for s in range(2):
            copies[s].wait_recv()
            passed.append(to_other(5 - k, s, offs[s] + (1 - 2 * steps[s][k][1]) * size, size))
    for copy in passed:
        copy.wait_recv()

    wlen = mixed.shape[0] // 2
    woffs = dp_offsets(dp, core, wlen)

    def mixed_copy(k, s):
        size = wlen >> (k + 1)
        partner, bit = steps[s][k]
        keep = s * wlen + woffs[s] // size * size
        give = keep + (1 - 2 * bit) * size
        slot = mixed_got.at[s, pl.ds(wlen - 2 * size, size)]
        return rcopy(mixed.at[pl.ds(pl.multiple_of(give, 8), size)], slot, w_send.at[s, k], w_recv.at[s, k], (partner, tensor)), keep, size

    def mixed_add(k):
        for s in range(2):
            copy, keep, size = mixed_copy(k, s)
            copy.wait_recv()
            rows = pl.ds(pl.multiple_of(keep, 8), size)
            mixed[rows, :] = mixed[rows, :] + mixed_got[s, wlen - 2 * size : wlen - size, :]

    def mixed_send(k):
        for s in range(2):
            mixed_copy(k, s)[0].start()

    for i in range(nblk):
        for j in range(nblk):
            if j < i:
                value = jnp.zeros((NB, NB), F32)
            else:
                value = whole[spots[i, j] : spots[i, j] + NB, :]
            inv_ref[i * NB : (i + 1) * NB, j * NB : (j + 1) * NB] = value

    def between(k):
        @pl.when(k == 0)
        def _():
            accumulate(3)
            accumulate(nz - 3)

        @pl.when(k == 1)
        def _():
            poll(nz // 2)
            accumulate(nz // 2)
            mixed_send(0)

        for phase, at in enumerate((4, 6, 7)):
            @pl.when(k == at)
            def _():
                mixed_add(phase)
                mixed_send(phase + 1)

    chol_inv(inv_ref, block, left, right, between)

    for k in range(0, n, 256):
        wide = inv_ref[k : k + 256, 0 : k + 256]
        high = wide.astype(BF16)
        inv_hi[k : k + 256, 0 : k + 256] = high
        inv_lo[k : k + 256, 0 : k + 256] = (wide - high.astype(F32)).astype(BF16)
    mixed_add(3)
    piece = wlen >> 4
    share = 2 * piece
    rows_at = [pl.multiple_of(s * wlen + woffs[s], 16) for s in range(2)]
    for s in range(2):
        wide = mixed[pl.ds(rows_at[s], piece), :]
        high = wide.astype(BF16)
        stacked[s * piece : (s + 1) * piece, :] = high
        stacked[share + s * piece : share + (s + 1) * piece, :] = (wide - high.astype(F32)).astype(BF16)
    def trans_part(k):
        e = k + 256
        both = mm_nt(stacked[:, 0:e], inv_hi[k:e, 0:e])
        trans = both[0:share, :] + both[share:, :] + mm_nt(stacked[0:share, 0:e], inv_lo[k:e, 0:e])
        squares = jnp.sum(trans * trans, axis=0, keepdims=True)
        for j in range(0, 256, NB):
            sq[(k + j) // NB : (k + j) // NB + 1, :] = squares[:, j : j + NB]
        half_part = trans.astype(BF16)
        for s in range(2):
            trans_ref[pl.ds(rows_at[s], piece), k:e] = half_part[s * piece : (s + 1) * piece, :]

    def gather_step(q, k):
        size = wlen >> (k + 1)
        copies = []
        for s in range(2):
            start = s * wlen + woffs[s] // size * size
            here = trans_ref.at[pl.ds(pl.multiple_of(start, 16), size), pl.ds(q * n // 2, n // 2)]
            copies.append(begin(rcopy(here, here, tr_send.at[q, s, k], tr_recv.at[q, s, k], (steps[s][k][0], tensor))))
        return copies

    def spread(source, slots, send, recv, devices):
        copies = []
        for d in range(1, len(devices)):
            copies.append(begin(rcopy(source, slots.at[d], send.at[d], recv.at[d], devices[d])))
        return copies

    def sum_of(source, slots, copies):
        out = source[...]
        for d in range(1, slots.shape[0]):
            copies[d - 1].wait_recv()
            out = out + slots[d]
        return out

    def ortho_part(i):
        count = all_ref.shape[0] // 4
        rows0 = i * count
        wide = all_ref[rows0 : rows0 + count, :]
        high = wide.astype(BF16)
        low = (wide - high.astype(F32)).astype(BF16)
        for k in range(0, n, 256):
            e = k + 256
            hi, lo = inv_hi[k:e, 0:e], inv_lo[k:e, 0:e]
            value = mm_nt(high[:, 0:e], hi) + (mm_nt(low[:, 0:e], hi) + mm_nt(high[:, 0:e], lo))
            ortho_ref[rows0 : rows0 + count, k:e] = value.astype(BF16)

    trans_part(0)
    trans_part(256)
    coming = [gather_step(0, 3)]
    trans_part(512)
    trans_part(768)
    coming.append(gather_step(1, 3))
    beside = spread(sq, sq_t, t_send, t_recv, tdev)
    for i, k in enumerate((2, 1, 0)):
        ortho_part(i)
        for q in range(2):
            for copy in coming[q]:
                copy.wait_recv()
            coming[q] = gather_step(q, k)
        if i == 0:
            sq_sum[...] = sum_of(sq, sq_t, beside)
            down = spread(sq_sum, sq_d, d_send, d_recv, ddev)
    ortho_part(3)
    scale = lax.rsqrt(sum_of(sq_sum, sq_d, down) + NORM_EPS)
    for copy in coming[0] + coming[1]:
        copy.wait_recv()
    for rows0 in range(0, trans_ref.shape[0], NB):
        for j in range(n // NB):
            value = trans_ref[rows0 : rows0 + NB, j * NB : (j + 1) * NB].astype(F32)
            basis_ref[rows0 : rows0 + NB, j * NB : (j + 1) * NB] = (value * scale[j : j + 1, :]).astype(BF16)
    for k in range(4):
        for s in range(2):
            mixed_copy(k, s)[0].wait_send()
    for r in range(nz):
        pair_copy(r).wait_send()
    for copy in pending:
        copy.wait_send()


def factor(projected, buffer):
    prows, n = projected.shape
    depth = buffer.shape[1]
    nblk = n // NB
    packed = nblk * (nblk + 1) // 2 * NB
    ntensor, ndp = lax.axis_size("tensor"), lax.axis_size("dp")
    nz = ntensor // 2
    rows = packed // 2
    last = rows // 2 // 16
    piece = -(-2 * last // (8 * nz)) * 8
    dma = pltpu.SemaphoreType.DMA
    vmem = pl.BlockSpec(memory_space=pltpu.VMEM)

    def f32(*shape):
        return pltpu.VMEM(shape, F32)

    def bf16(*shape):
        return pltpu.VMEM(shape, BF16)

    return pl.pallas_call(
        factor_kernel,
        out_shape=[
            jax.ShapeDtypeStruct((prows * ntensor, n), BF16),
            jax.ShapeDtypeStruct((depth, n), BF16),
            jax.ShapeDtypeStruct((depth, n), BF16),
        ],
        in_specs=[vmem] * 2,
        out_specs=[vmem] * 3,
        scratch_shapes=[
            f32(n, n), f32(prows * ntensor, n), bf16(6 * NB, n), bf16(6 * NB, n),
            bf16(n, n), bf16(n, n), bf16(2 * depth // ndp, n),
            f32(packed, NB), f32(rows, NB), f32(2, rows // 2, NB),
            f32(piece * nz, NB), f32(nz, piece, NB), f32(piece * nz, NB), f32(packed, NB),
            f32(NB, NB), f32(depth, n), f32(2, depth // 2, n),
            f32(nblk, NB), f32(ntensor, nblk, NB), f32(ndp, nblk, NB), f32(nblk, NB),
            dma((2, 6)), dma((2, 6)), dma((2, 4)), dma((2, 4)), dma((nz,)), dma((nz,)),
            dma((2, 4)), dma((2, 4)), dma((nz,)), dma((nz,)),
            dma((nz // 2,)), dma((nz // 2,)), dma((nz // 2,)), dma((nz // 2,)), dma((nz,)), dma((nz,)),
            dma((2, 4)), dma((2, 4)), dma((2, 2, 4)), dma((2, 2, 4)),
            dma((ntensor,)), dma((ntensor,)), dma((ndp,)), dma((ndp,)),
        ],
        compiler_params=pltpu.CompilerParams(
            vmem_limit_bytes=58 << 20, collective_id=1, has_side_effects=True
        ),
        cost_estimate=pl.CostEstimate(flops=60_000_000_000, bytes_accessed=24 << 20, transcendentals=0),
        name="factor",
    )(projected, buffer)


def project_kernel(buf_ref, share_ref, out_ref, basis, natural, part, swapped, acc, ring, ag_send, ag_recv, sw_send, sw_recv, ring_send, ring_recv):
    dp, tensor = lax.axis_index("dp"), lax.axis_index("tensor")
    ndp, nz = lax.axis_size("dp"), lax.axis_size("tensor") // 2
    core, z = lax.rem(tensor, 2), tensor // 2
    other = (dp, tensor + 1 - 2 * core)
    after = (dp, lax.rem(z + 1 - 2 * core + nz, nz) * 2 + core)
    before = (dp, lax.rem(z - 1 + 2 * core + nz, nz) * 2 + core)
    steps = dp_steps(core)
    enter([(partner, tensor) for partner, _ in steps[0]] + [other, after, before])
    pending = []

    def begin(copy):
        copy.start()
        pending.append(copy)
        return copy

    share = share_ref.shape[0] // 2
    length = basis.shape[1] // 2
    offs = dp_offsets(dp, core, length)
    half = share // 2
    for q in range(2):
        for s in range(2):
            basis[q, pl.ds(pl.multiple_of(s * length + offs[s], 16), half), :] = share_ref[
                q * share + s * half : q * share + (s + 1) * half, :
            ]

    def gather_step(q, k):
        size = length >> (k + 1)
        copies = []
        for s in range(2):
            here = basis.at[q, pl.ds(pl.multiple_of(s * length + offs[s] // size * size, 16), size)]
            copies.append(begin(rcopy(here, here, ag_send.at[q, s, k], ag_recv.at[q, s, k], (steps[s][k][0], tensor))))
        return copies

    def arrive(copies):
        for copy in copies:
            copy.wait_recv()

    def sort(q):
        for d in range(ndp):
            there = dp_offsets(d, core, length)
            for s in range(2):
                rows0 = d * share + s * half
                natural[q, rows0 : rows0 + half, :] = basis[q, pl.ds(pl.multiple_of(s * length + there[s], 16), half), :]

    coming = [gather_step(q, 3) for q in range(2)]
    for k in (2, 1, 0):
        for q in range(2):
            arrive(coming[q])
            coming[q] = gather_step(q, k)
    arrive(coming[0])
    sort(0)

    chunk = buf_ref.shape[0] // nz
    rows = chunk // 2
    mine = pl.multiple_of(core * rows, 8)
    theirs = pl.multiple_of((1 - core) * rows, 8)
    columns = out_ref.shape[1] // 2

    def swap(r, q):
        here = pl.ds(q * columns, columns)
        return rcopy(part.at[r, pl.ds(theirs, rows), here], swapped.at[r, :, here], sw_send.at[q, r], sw_recv.at[q, r], other)

    def compute(q, *places):
        for r in places:
            rows0 = pl.multiple_of(lax.rem(z + r, nz) * chunk, 16)
            part[r, :, q * columns : (q + 1) * columns] = mm_nt(buf_ref[pl.ds(rows0, chunk), :], natural[q])
            begin(swap(r, q))

    def term(r, q):
        here = slice(q * columns, (q + 1) * columns)
        return part[r, pl.ds(mine, rows), here] + swapped[r, :, here]

    last = [None, None]

    def ring_step(q, s):
        r = core * (1 + s) + (1 - core) * (nz - 1 - s)
        swap(r, q).wait_recv()
        value = term(r, q)
        if s > 0:
            last[q].wait_recv()
            value = value + ring[s - 1, q]
        acc[s, q] = value
        last[q] = begin(rcopy(acc.at[s, q], ring.at[s, q], ring_send.at[s, q], ring_recv.at[s, q], after))

    pairs = [(r, nz - r) for r in range(1, nz // 2)] + [(nz // 2, 0)]
    compute(0, *pairs[0])
    compute(0, *pairs[1])
    ring_step(0, 0)
    arrive(coming[1])
    sort(1)
    compute(1, *pairs[0])
    ring_step(0, 1)
    compute(1, *pairs[1])
    ring_step(1, 0)
    for i in range(2, nz // 2):
        compute(0, *pairs[i])
        ring_step(0, i)
        compute(1, *pairs[i])
        ring_step(1, i - 1)
    for i in range(nz // 2, nz - 1):
        ring_step(0, i)
        ring_step(1, i - 1)
    ring_step(1, nz - 2)
    done = []
    for q in range(2):
        swap(0, q).wait_recv()
        value = term(0, q)
        last[q].wait_recv()
        done.append(value + ring[nz - 2, q])
    for j in range(0, 2 * columns, NB):
        k = j // 2
        out_ref[:, j : j + NB] = jnp.concatenate(
            [done[q][:, k + i * share : k + (i + 1) * share] for i in range(NB // 2 // share) for q in range(2)], axis=1
        )
    for copy in pending:
        copy.wait_send()


def project(buffer, share):
    nz = lax.axis_size("tensor") // 2
    n = share.shape[0] * lax.axis_size("dp")
    depth = share.shape[1]
    rows = buffer.shape[0] // nz // 2
    dma = pltpu.SemaphoreType.DMA
    vmem = pl.BlockSpec(memory_space=pltpu.VMEM)
    return pl.pallas_call(
        project_kernel,
        out_shape=jax.ShapeDtypeStruct((rows, n), F32),
        in_specs=[vmem] * 2,
        out_specs=vmem,
        scratch_shapes=[
            pltpu.VMEM((2, n // 2, depth), BF16), pltpu.VMEM((2, n // 2, depth), BF16),
            pltpu.VMEM((nz, 2 * rows, n), F32), pltpu.VMEM((nz, rows, n), F32),
            pltpu.VMEM((nz - 1, 2, rows, n // 2), F32), pltpu.VMEM((nz - 1, 2, rows, n // 2), F32),
            dma((2, 2, 4)), dma((2, 2, 4)), dma((2, nz)), dma((2, nz)), dma((nz - 1, 2)), dma((nz - 1, 2)),
        ],
        compiler_params=pltpu.CompilerParams(
            vmem_limit_bytes=48 << 20, collective_id=3, has_side_effects=True
        ),
        cost_estimate=pl.CostEstimate(flops=20_000_000_000, bytes_accessed=16 << 20, transcendentals=0),
        name="project",
    )(buffer, share)


def output_kernel(scale_up, ortho_ref, trans_ref, basis_ref, buf_ref, new_ref, update_ref):
    ortho = ortho_ref[...]
    for k in range(0, trans_ref.shape[0], 512):
        feedback = mm_nt(ortho, trans_ref[k : k + 512, :])
        new_ref[:, k : k + 512] = (buf_ref[:, k : k + 512].astype(F32) - FEEDBACK_SHARE * feedback).astype(BF16)
        product = mm_nt(ortho, basis_ref[k : k + 512, :])
        update_ref[:, k : k + 512] = (-scale_up * product).astype(BF16)


def outputs(ortho, trans, basis, buffer, scale_up):
    rows, depth = buffer.shape
    n = ortho.shape[1]
    tile = rows // 4
    whole = pl.BlockSpec(memory_space=pltpu.VMEM)
    strip = pl.BlockSpec((tile, depth), lambda i: (i, 0))
    return pl.pallas_call(
        functools.partial(output_kernel, scale_up),
        grid=(rows // tile,),
        out_shape=[jax.ShapeDtypeStruct((rows, depth), BF16)] * 2,
        in_specs=[pl.BlockSpec((tile, n), lambda i: (i, 0)), whole, whole, strip],
        out_specs=[strip, strip],
        compiler_params=pltpu.CompilerParams(vmem_limit_bytes=40 << 20),
        cost_estimate=pl.CostEstimate(flops=8_000_000_000, bytes_accessed=20 << 20, transcendentals=0),
        name="outputs",
    )(ortho, trans, basis, buffer)


def body(buffer, old_basis):
    groups = lax.axis_size("tensor")
    share = old_basis.shape[1]
    rank = share * lax.axis_size("dp")
    projected = project(buffer, old_basis.T)
    ortho_all, trans_all, basis_all = factor(projected, buffer)
    new_basis = lax.dynamic_slice_in_dim(basis_all, lax.axis_index("dp") * share, share, axis=1)
    scale_up = math.sqrt(
        buffer.shape[0] * lax.axis_size("dp") * buffer.shape[1] * groups / rank
    )
    new_buffer, weight_update = outputs(ortho_all, trans_all, basis_all, buffer, scale_up)
    return (new_buffer, weight_update, new_basis)


def solution(mesh):
    in_specs = (P("dp", "tensor"), P("tensor", "dp"))
    out_specs = (P("dp", "tensor"), P("dp", "tensor"), P("tensor", "dp"))
    return jax.shard_map(body, mesh=mesh, in_specs=in_specs, out_specs=out_specs, check_vma=False)
```

```python
import functools
import math

import jax
import jax.numpy as jnp
from jax import lax
from jax.experimental import pallas as pl
from jax.experimental.pallas import tpu as pltpu
from jax.sharding import PartitionSpec as P

NORM_EPS = 1e-06
FEEDBACK_SHARE = 0.05
HI = lax.Precision.HIGHEST
F32 = jnp.float32
BF16 = jnp.bfloat16
NB = 128
MP = 32


def mm_tn(a, b, precision=None):
    return lax.dot_general(
        a, b, (((0,), (0,)), ((), ())), precision=precision, preferred_element_type=F32
    )


def mm_nn(a, b, precision=None):
    return lax.dot_general(
        a, b, (((1,), (0,)), ((), ())), precision=precision, preferred_element_type=F32
    )


def mm_nt(a, b, precision=None):
    return lax.dot_general(
        a, b, (((1,), (1,)), ((), ())), precision=precision, preferred_element_type=F32
    )


def three(x):
    h = x.astype(BF16)
    rest = x - h.astype(F32)
    m = rest.astype(BF16)
    return h, m, (rest - m.astype(F32)).astype(BF16)


def eliminate_rows(rows, r0):
    lane = lax.broadcasted_iota(jnp.int32, (8, NB), 1)
    row = lax.broadcasted_iota(jnp.int32, (8, NB), 0)
    groups = MP // 8
    parts = [rows[8 * g : 8 * g + 8, :] for g in range(groups)]
    cols = [
        [jnp.broadcast_to(parts[g][:, r0 + c : r0 + c + 1], (8, NB)) if g >= c // 8 else None for g in range(groups)]
        for c in range(MP)
    ]
    scales = [jnp.zeros((8, NB), F32) for _ in range(groups)]

    def spread(value, i):
        return jnp.broadcast_to(value[i : i + 1, :], (8, NB))

    for c in range(MP):
        own, at = c // 8, c % 8
        rs = lax.rsqrt(spread(cols[c][own], at))
        inv = rs * rs
        f = [None] * groups
        for g in range(own, groups):
            f[g] = cols[c][g] * inv
        f[own] = jnp.where(row > at, f[own], 0.0)
        for c2 in range(c + 1, MP):
            e = spread(cols[c][c2 // 8], c2 % 8)
            for g in range(c2 // 8, groups):
                cols[c2][g] = cols[c2][g] - f[g] * e
        pivot = jnp.where(lane == r0 + c, 1.0, spread(parts[own], at))
        for g in range(groups):
            if g < own:
                parts[g] = jnp.where(lane == r0 + c, 0.0, parts[g])
            else:
                kept = jnp.where(lane == r0 + c, 0.0, parts[g])
                if g == own:
                    kept = jnp.where(row == at, pivot, kept)
                parts[g] = kept - f[g] * pivot
        scales[own] = jnp.where(row == at, rs, scales[own])
    return jnp.concatenate([p * v for p, v in zip(parts, scales)], axis=0)


def eliminate_block(block):
    lane = lax.broadcasted_iota(jnp.int32, (NB, NB), 1)
    for r0 in range(0, NB, MP):
        rows = eliminate_rows(block[r0 : r0 + MP, :], r0)
        block[r0 : r0 + MP, :] = rows
        if r0 + MP < NB:
            h, m, l = three(rows)
            left = jnp.concatenate([h, h, m, h, l, m], axis=0)
            right = jnp.concatenate([h, m, h, l, h, m], axis=0)
            update = mm_tn(left, right)[r0 + MP :, :]
            below = lane[r0 + MP :, :]
            old = jnp.where((below >= r0) & (below < r0 + MP), 0.0, block[r0 + MP :, :])
            block[r0 + MP :, :] = old - update


def chol_inv(out_ref, block, left, right, between):
    n = out_ref.shape[0]
    nblk = n // NB
    lane = lax.broadcasted_iota(jnp.int32, (NB, NB), 1)
    row = lax.broadcasted_iota(jnp.int32, (NB, NB), 0)

    def step(k, _):
        between(k)
        k0 = pl.multiple_of(k * NB, NB)
        block[...] = out_ref[pl.ds(k0, NB), pl.ds(k0, NB)]
        eliminate_block(block)
        linv = jnp.where(lane <= row, block[...], 0.0)
        out_ref[pl.ds(k0, NB), :] = mm_nn(linv, out_ref[pl.ds(k0, NB), :], HI)
        out_ref[pl.ds(k0, NB), pl.ds(k0, NB)] = linv
        h, m, l = three(out_ref[pl.ds(k0, NB), :])
        for j, (a, b) in enumerate(zip((h, h, m, h, l, m), (h, m, h, l, h, m))):
            left[j * NB : (j + 1) * NB, :] = a
            right[j * NB : (j + 1) * NB, :] = b

        def below(i0, size):
            out_ref[pl.ds(i0, size), pl.ds(k0, NB)] = jnp.zeros((size, NB), F32)
            out_ref[pl.ds(i0, size), :] = out_ref[pl.ds(i0, size), :] - mm_tn(
                left[:, pl.ds(i0, size)], right[...]
            )

        @pl.when(lax.rem(k, 2) == 0)
        def _():
            below(pl.multiple_of(k0 + NB, NB), NB)

        def pair(i, _):
            below(pl.multiple_of(i * 2 * NB, 2 * NB), 2 * NB)
            return 0

        lax.fori_loop(k // 2 + 1, nblk // 2, pair, 0)
        return 0

    lax.fori_loop(0, nblk, step, 0)
    for k0 in range(0, n - NB, NB):
        out_ref[k0 : k0 + NB, k0 + NB :] = jnp.zeros((NB, n - k0 - NB), F32)


def rcopy(src, dst, send_sem, recv_sem, device):
    return pltpu.make_async_remote_copy(
        src_ref=src, dst_ref=dst, send_sem=send_sem, recv_sem=recv_sem,
        device_id=device, device_id_type=pl.DeviceIdType.MESH,
    )


def dp_steps(core):
    dp = lax.axis_index("dp")
    x, y = lax.rem(dp, 4), dp // 4

    def pairs(v):
        gray, high = lax.rem(v + v // 2, 2), v // 2
        near, far = v + 1 - 2 * lax.rem(v, 2), 3 - v
        other = 1 - core
        return (
            (other * near + core * far, other * gray + core * high),
            (other * far + core * near, other * high + core * gray),
        )

    xs = [(y * 4 + v, bit) for v, bit in pairs(x)]
    ys = [(v * 4 + x, bit) for v, bit in pairs(y)]
    return (xs + ys, ys + xs)


def enter(devices):
    barrier = pltpu.get_barrier_semaphore()
    for device in devices:
        pl.semaphore_signal(barrier, inc=1, device_id=device, device_id_type=pl.DeviceIdType.MESH)
    pl.semaphore_wait(barrier, len(devices))


def dp_offsets(dp, core, length):
    def bits(v):
        gray, high = (v + v // 2) % 2, v // 2
        other = 1 - core
        return [other * gray + core * high, other * high + core * gray]

    xs, ys = bits(dp % 4), bits(dp // 4)
    out = []
    for order in (xs + ys, ys + xs):
        at, size = 0, length
        for bit in order:
            size //= 2
            at = at + bit * size
        out.append(at)
    return out


def factor_kernel(
    p_ref, buf_hbm, ortho_hbm, trans_ref, basis_ref, buf_ref, ortho_ref, inv_ref, all_ref, left, right, inv_hi, inv_lo, stacked, part, half, got, sums, zgot, zsums, whole, block, mixed, mixed_got, sq, sq_t, sq_d, sq_sum, core_send, core_recv, dp_send, dp_recv, z_send, z_recv, ag_send, ag_recv, zag_send, zag_recv, plus_send, plus_recv, minus_send, minus_recv, pair_send, pair_recv, w_send, w_recv, tr_send, tr_recv, t_send, t_recv, d_send, d_recv, local_sem,
):
    dp, tensor = lax.axis_index("dp"), lax.axis_index("tensor")
    core, z = lax.rem(tensor, 2), tensor // 2
    nz = lax.axis_size("tensor") // 2
    other = (dp, tensor + 1 - 2 * core)
    steps = dp_steps(core)
    ndp, ntensor = lax.axis_size("dp"), 2 * nz
    zdev = [(dp, lax.rem(z + d, nz) * 2 + core) for d in range(nz)]
    tdev = [(dp, lax.rem(tensor + d, ntensor)) for d in range(ntensor)]
    ddev = [(lax.rem(dp + d, ndp), tensor) for d in range(ndp)]
    load = pltpu.make_async_copy(buf_hbm, buf_ref, local_sem.at[0])
    load.start()
    enter(tdev[1:] + ddev[1:])
    pending = []

    prows, n = p_ref.shape

    places = [lax.rem(z + (1 - 2 * core) * r + nz, nz) for r in range(nz)]
    ahead, behind = [(dp, places[r] * 2 + core) for r in (1, nz - 1)]

    own_at = [pl.multiple_of((places[r] * 2 + core) * prows, 8) for r in range(nz)]

    def region(r):
        return all_ref.at[pl.ds(own_at[r], prows)]

    def begin(copy):
        copy.start()
        pending.append(copy)
        return copy

    def pass_on(j):
        plus = region(nz - j if j else 0)
        begin(rcopy(plus, plus, plus_send.at[j], plus_recv.at[j], ahead))
        if j < nz // 2 - 1:
            minus = region(j)
            begin(rcopy(minus, minus, minus_send.at[j], minus_recv.at[j], behind))

    def pair_copy(r):
        here = region(r)
        return rcopy(here, here, pair_send.at[r], pair_recv.at[r], other)

    def across(r):
        pair_copy(r).start()

    def poll(j):
        here = region(nz - j)
        rcopy(here, here, plus_send.at[j - 1], plus_recv.at[j - 1], ahead).wait_recv()
        if j < nz // 2:
            here = region(j)
            rcopy(here, here, minus_send.at[j - 1], minus_recv.at[j - 1], behind).wait_recv()
            pass_on(j)
            across(j)
        across(nz - j)

    chunk = 2 * prows
    chunk_at = [pl.multiple_of(places[r] * chunk, 16) for r in range(nz)]

    def accumulate(r):
        here = region(r)
        rcopy(here, here, pair_send.at[r], pair_recv.at[(nz - r) % nz], other).wait_recv()
        rows0 = chunk_at[r]
        wide = all_ref[pl.ds(rows0, chunk), :]
        high = wide.astype(BF16)
        low = (wide - high.astype(F32)).astype(BF16)

        for i0 in range(0, mixed.shape[0], 256):
            columns = buf_ref[pl.ds(rows0, chunk), i0 : i0 + 256]
            for k in range(0, n, 256):
                value = mm_tn(columns, high[:, k : k + 256]) + mm_tn(columns, low[:, k : k + 256])
                if r:
                    value = value + mixed[i0 : i0 + 256, k : k + 256]
                mixed[i0 : i0 + 256, k : k + 256] = value

    own_rows = pl.multiple_of(tensor * prows, 8)
    all_ref[pl.ds(own_rows, prows), :] = p_ref[...]
    pass_on(0)
    across(0)

    nblk = n // NB
    order = [[0, 1, nblk - 2, nblk - 1], list(range(2, nblk - 2))]
    spots = {}
    for i in order[0] + order[1]:
        for j in range(i, nblk):
            spots[i, j] = len(spots) * NB
    rows = len(spots) * NB // 2
    mine = pl.multiple_of(core * rows, 8)
    theirs = pl.multiple_of((1 - core) * rows, 8)
    deep = -(-prows // 16) * 16
    padded = jnp.concatenate([p_ref[...], jnp.zeros((deep - prows, n), F32)], axis=0)
    h, m, l = three(padded)
    for j, (a, b) in enumerate(zip((h, h, m, h, l, m), (h, m, h, l, h, m))):
        left[j * deep : (j + 1) * deep, :] = a
        right[j * deep : (j + 1) * deep, :] = b

    def gram_half(which):
        for i in order[which][::2]:
            i0 = i * NB
            prod = mm_tn(left[0 : 6 * deep, i0 : i0 + 2 * NB], right[0 : 6 * deep, i0:])
            for i2 in (i, i + 1):
                for j in range(i2, nblk):
                    at = spots[i2, j]
                    part[at : at + NB, :] = prod[(i2 - i) * NB : (i2 - i + 1) * NB, (j - i) * NB : (j - i + 1) * NB]

    for c in range(2):
        @pl.when(core == c)
        def _():
            gram_half(1 - c)

    swap = begin(rcopy(part.at[pl.ds(theirs, rows)], half, core_send.at[0, 0], core_recv.at[0, 0], other))
    for c in range(2):
        @pl.when(core == c)
        def _():
            gram_half(c)

    swap.wait_recv()
    half[...] = half[...] + part[pl.ds(mine, rows), :]

    length = rows // 2
    offs = [0, length]
    trail = []
    size = length
    got_at = 0
    for k in range(4):
        size //= 2
        copies = []
        for s in range(2):
            partner, bit = steps[s][k]
            keep = pl.multiple_of(offs[s] + bit * size, 8)
            give = pl.multiple_of(offs[s] + (1 - bit) * size, 8)
            copies.append(begin(rcopy(half.at[pl.ds(give, size)], got.at[s, pl.ds(got_at, size)], dp_send.at[s, k], dp_recv.at[s, k], (partner, tensor))))
            offs[s] = keep
        if k == 0:
            load.wait()
            accumulate(0)
        for s in range(2):
            copies[s].wait_recv()
            half[pl.ds(offs[s], size), :] = half[pl.ds(offs[s], size), :] + got[s, pl.ds(got_at, size), :]
        if k == 0:
            poll(1)
        trail.append((size, list(offs)))
        got_at += size

    sums[0:size, :] = half[pl.ds(offs[0], size), :]
    sums[size : 2 * size, :] = half[pl.ds(offs[1], size), :]
    piece = sums.shape[0] // nz
    if sums.shape[0] > 2 * size:
        sums[2 * size :, :] = jnp.zeros((sums.shape[0] - 2 * size, NB), F32)
    copies = []
    for d in range(1, nz):
        zto = lax.rem(z + d, nz)
        copies.append(begin(rcopy(sums.at[pl.ds(pl.multiple_of(zto * piece, 8), piece)], zgot.at[d], z_send.at[d], z_recv.at[d], zdev[d])))
    own = pl.multiple_of(z * piece, 8)
    total = sums[pl.ds(own, piece), :]
    for d in range(1, nz):
        copies[d - 1].wait_recv()
        total = total + zgot[d]
    zsums[pl.ds(own, piece), :] = total
    copies = []
    for d in range(1, nz):
        copies.append(begin(rcopy(zsums.at[pl.ds(own, piece)], zsums.at[pl.ds(own, piece)], zag_send.at[d], zag_recv.at[d], zdev[d])))
    for copy in copies:
        copy.wait_recv()
    poll(2)

    def to_other(stage, s, start, count):
        here = whole.at[pl.ds(pl.multiple_of(mine + start, 8), count)]
        return begin(rcopy(here, here, core_send.at[s, stage], core_recv.at[s, stage], other))

    passed = []
    for s in range(2):
        whole[pl.ds(pl.multiple_of(mine + offs[s], 8), size), :] = zsums[s * size : (s + 1) * size, :]
        passed.append(to_other(1, s, offs[s], size))
    for k in reversed(range(4)):
        size, offs = trail[k]
        copies = []
        for s in range(2):
            here = whole.at[pl.ds(pl.multiple_of(mine + offs[s], 8), size)]
            copies.append(begin(rcopy(here, here, ag_send.at[s, k], ag_recv.at[s, k], (steps[s][k][0], tensor))))
        if k == 3:
            accumulate(1)
        elif k == 2:
            accumulate(nz - 1)
        elif k == 0:
            poll(3)
            accumulate(2)
            accumulate(nz - 2)
        for s in range(2):
            copies[s].wait_recv()
            passed.append(to_other(5 - k, s, offs[s] + (1 - 2 * steps[s][k][1]) * size, size))
    for copy in passed:
        copy.wait_recv()

    wlen = mixed.shape[0] // 2
    woffs = dp_offsets(dp, core, wlen)

    def mixed_copy(k, s):
        size = wlen >> (k + 1)
        partner, bit = steps[s][k]
        keep = s * wlen + woffs[s] // size * size
        give = keep + (1 - 2 * bit) * size
        slot = mixed_got.at[s, pl.ds(wlen - 2 * size, size)]
        return rcopy(mixed.at[pl.ds(pl.multiple_of(give, 8), size)], slot, w_send.at[s, k], w_recv.at[s, k], (partner, tensor)), keep, size

    def mixed_add(k):
        for s in range(2):
            copy, keep, size = mixed_copy(k, s)
            copy.wait_recv()
            rows = pl.ds(pl.multiple_of(keep, 8), size)
            mixed[rows, :] = mixed[rows, :] + mixed_got[s, wlen - 2 * size : wlen - size, :]

    def mixed_send(k):
        for s in range(2):
            mixed_copy(k, s)[0].start()

    for i in range(nblk):
        for j in range(nblk):
            if j < i:
                value = jnp.zeros((NB, NB), F32)
            else:
                value = whole[spots[i, j] : spots[i, j] + NB, :]
            inv_ref[i * NB : (i + 1) * NB, j * NB : (j + 1) * NB] = value

    def between(k):
        @pl.when(k == 0)
        def _():
            accumulate(3)
            accumulate(nz - 3)

        @pl.when(k == 1)
        def _():
            poll(nz // 2)
            accumulate(nz // 2)
            mixed_send(0)

        for phase, at in enumerate((4, 6, 7)):
            @pl.when(k == at)
            def _():
                mixed_add(phase)
                mixed_send(phase + 1)

    chol_inv(inv_ref, block, left, right, between)

    for k in range(0, n, 256):
        wide = inv_ref[k : k + 256, 0 : k + 256]
        high = wide.astype(BF16)
        inv_hi[k : k + 256, 0 : k + 256] = high
        inv_lo[k : k + 256, 0 : k + 256] = (wide - high.astype(F32)).astype(BF16)
    mixed_add(3)
    piece = wlen >> 4
    share = 2 * piece
    rows_at = [pl.multiple_of(s * wlen + woffs[s], 16) for s in range(2)]
    for s in range(2):
        wide = mixed[pl.ds(rows_at[s], piece), :]
        high = wide.astype(BF16)
        stacked[s * piece : (s + 1) * piece, :] = high
        stacked[share + s * piece : share + (s + 1) * piece, :] = (wide - high.astype(F32)).astype(BF16)
    def trans_part(k):
        e = k + 256
        both = mm_nt(stacked[:, 0:e], inv_hi[k:e, 0:e])
        trans = both[0:share, :] + both[share:, :] + mm_nt(stacked[0:share, 0:e], inv_lo[k:e, 0:e])
        squares = jnp.sum(trans * trans, axis=0, keepdims=True)
        for j in range(0, 256, NB):
            sq[(k + j) // NB : (k + j) // NB + 1, :] = squares[:, j : j + NB]
        half_part = trans.astype(BF16)
        for s in range(2):
            trans_ref[pl.ds(rows_at[s], piece), k:e] = half_part[s * piece : (s + 1) * piece, :]

    def gather_step(q, k):
        size = wlen >> (k + 1)
        copies = []
        for s in range(2):
            start = s * wlen + woffs[s] // size * size
            here = trans_ref.at[pl.ds(pl.multiple_of(start, 16), size), pl.ds(q * n // 2, n // 2)]
            copies.append(begin(rcopy(here, here, tr_send.at[q, s, k], tr_recv.at[q, s, k], (steps[s][k][0], tensor))))
        return copies

    def spread(source, slots, send, recv, devices):
        copies = []
        for d in range(1, len(devices)):
            copies.append(begin(rcopy(source, slots.at[d], send.at[d], recv.at[d], devices[d])))
        return copies

    def sum_of(source, slots, copies):
        out = source[...]
        for d in range(1, slots.shape[0]):
            copies[d - 1].wait_recv()
            out = out + slots[d]
        return out

    stores = []

    def ortho_part(i):
        count = all_ref.shape[0] // 4
        rows0 = i * count
        wide = all_ref[rows0 : rows0 + count, :]
        high = wide.astype(BF16)
        low = (wide - high.astype(F32)).astype(BF16)
        for k in range(0, n, 256):
            e = k + 256
            hi, lo = inv_hi[k:e, 0:e], inv_lo[k:e, 0:e]
            value = mm_nt(high[:, 0:e], hi) + (mm_nt(low[:, 0:e], hi) + mm_nt(high[:, 0:e], lo))
            ortho_ref[rows0 : rows0 + count, k:e] = value.astype(BF16)
        here = pl.ds(rows0, count)
        store = pltpu.make_async_copy(ortho_ref.at[here], ortho_hbm.at[here], local_sem.at[1 + i])
        store.start()
        stores.append(store)

    trans_part(0)
    trans_part(256)
    coming = [gather_step(0, 3)]
    trans_part(512)
    trans_part(768)
    coming.append(gather_step(1, 3))
    beside = spread(sq, sq_t, t_send, t_recv, tdev)
    for i, k in enumerate((2, 1, 0)):
        ortho_part(i)
        for q in range(2):
            for copy in coming[q]:
                copy.wait_recv()
            coming[q] = gather_step(q, k)
        if i == 0:
            sq_sum[...] = sum_of(sq, sq_t, beside)
            down = spread(sq_sum, sq_d, d_send, d_recv, ddev)
    ortho_part(3)
    scale = lax.rsqrt(sum_of(sq_sum, sq_d, down) + NORM_EPS)
    for copy in coming[0] + coming[1]:
        copy.wait_recv()
    for rows0 in range(0, trans_ref.shape[0], NB):
        for j in range(n // NB):
            value = trans_ref[rows0 : rows0 + NB, j * NB : (j + 1) * NB].astype(F32)
            basis_ref[rows0 : rows0 + NB, j * NB : (j + 1) * NB] = (value * scale[j : j + 1, :]).astype(BF16)
    for k in range(4):
        for s in range(2):
            mixed_copy(k, s)[0].wait_send()
    for store in stores:
        store.wait()
    for r in range(nz):
        pair_copy(r).wait_send()
    for copy in pending:
        copy.wait_send()


def factor(projected, buffer):
    prows, n = projected.shape
    depth = buffer.shape[1]
    nblk = n // NB
    packed = nblk * (nblk + 1) // 2 * NB
    ntensor, ndp = lax.axis_size("tensor"), lax.axis_size("dp")
    nz = ntensor // 2
    rows = packed // 2
    last = rows // 2 // 16
    piece = -(-2 * last // (8 * nz)) * 8
    dma = pltpu.SemaphoreType.DMA
    vmem = pl.BlockSpec(memory_space=pltpu.VMEM)

    def f32(*shape):
        return pltpu.VMEM(shape, F32)

    def bf16(*shape):
        return pltpu.VMEM(shape, BF16)

    return pl.pallas_call(
        factor_kernel,
        out_shape=[
            jax.ShapeDtypeStruct((prows * ntensor, n), BF16),
            jax.ShapeDtypeStruct((depth, n), BF16),
            jax.ShapeDtypeStruct((depth, n), BF16),
        ],
        in_specs=[vmem, pl.BlockSpec(memory_space=pl.ANY)],
        out_specs=[pl.BlockSpec(memory_space=pl.ANY), vmem, vmem],
        scratch_shapes=[
            bf16(*buffer.shape), bf16(prows * ntensor, n), f32(n, n), f32(prows * ntensor, n), bf16(6 * NB, n), bf16(6 * NB, n),
            bf16(n, n), bf16(n, n), bf16(2 * depth // ndp, n),
            f32(packed, NB), f32(rows, NB), f32(2, rows // 2, NB),
            f32(piece * nz, NB), f32(nz, piece, NB), f32(piece * nz, NB), f32(packed, NB),
            f32(NB, NB), f32(depth, n), f32(2, depth // 2, n),
            f32(nblk, NB), f32(ntensor, nblk, NB), f32(ndp, nblk, NB), f32(nblk, NB),
            dma((2, 6)), dma((2, 6)), dma((2, 4)), dma((2, 4)), dma((nz,)), dma((nz,)),
            dma((2, 4)), dma((2, 4)), dma((nz,)), dma((nz,)),
            dma((nz // 2,)), dma((nz // 2,)), dma((nz // 2,)), dma((nz // 2,)), dma((nz,)), dma((nz,)),
            dma((2, 4)), dma((2, 4)), dma((2, 2, 4)), dma((2, 2, 4)),
            dma((ntensor,)), dma((ntensor,)), dma((ndp,)), dma((ndp,)), dma((5,)),
        ],
        compiler_params=pltpu.CompilerParams(
            vmem_limit_bytes=58 << 20, collective_id=1, has_side_effects=True
        ),
        cost_estimate=pl.CostEstimate(flops=60_000_000_000, bytes_accessed=24 << 20, transcendentals=0),
        name="factor",
    )(projected, buffer)


def project_kernel(buf_hbm, share_ref, out_ref, buf_ref, basis, natural, part, swapped, acc, ring, load_sem, ag_send, ag_recv, sw_send, sw_recv, ring_send, ring_recv):
    dp, tensor = lax.axis_index("dp"), lax.axis_index("tensor")
    ndp, nz = lax.axis_size("dp"), lax.axis_size("tensor") // 2
    core, z = lax.rem(tensor, 2), tensor // 2
    other = (dp, tensor + 1 - 2 * core)
    after = (dp, lax.rem(z + 1 - 2 * core + nz, nz) * 2 + core)
    before = (dp, lax.rem(z - 1 + 2 * core + nz, nz) * 2 + core)
    steps = dp_steps(core)
    load = pltpu.make_async_copy(buf_hbm, buf_ref, load_sem.at[0])
    load.start()
    enter([(partner, tensor) for partner, _ in steps[0]] + [other, after, before])
    pending = []

    def begin(copy):
        copy.start()
        pending.append(copy)
        return copy

    share = share_ref.shape[0] // 2
    length = basis.shape[1] // 2
    offs = dp_offsets(dp, core, length)
    half = share // 2
    for q in range(2):
        for s in range(2):
            basis[q, pl.ds(pl.multiple_of(s * length + offs[s], 16), half), :] = share_ref[
                q * share + s * half : q * share + (s + 1) * half, :
            ]

    def gather_step(q, k):
        size = length >> (k + 1)
        copies = []
        for s in range(2):
            here = basis.at[q, pl.ds(pl.multiple_of(s * length + offs[s] // size * size, 16), size)]
            copies.append(begin(rcopy(here, here, ag_send.at[q, s, k], ag_recv.at[q, s, k], (steps[s][k][0], tensor))))
        return copies

    def arrive(copies):
        for copy in copies:
            copy.wait_recv()

    def sort(q):
        for d in range(ndp):
            there = dp_offsets(d, core, length)
            for s in range(2):
                rows0 = d * share + s * half
                natural[q, rows0 : rows0 + half, :] = basis[q, pl.ds(pl.multiple_of(s * length + there[s], 16), half), :]

    coming = [gather_step(q, 3) for q in range(2)]
    for k in (2, 1, 0):
        for q in range(2):
            arrive(coming[q])
            coming[q] = gather_step(q, k)
    arrive(coming[0])
    sort(0)

    chunk = buf_ref.shape[0] // nz
    rows = chunk // 2
    mine = pl.multiple_of(core * rows, 8)
    theirs = pl.multiple_of((1 - core) * rows, 8)
    columns = out_ref.shape[1] // 2

    def swap(r, q):
        here = pl.ds(q * columns, columns)
        return rcopy(part.at[r, pl.ds(theirs, rows), here], swapped.at[r, :, here], sw_send.at[q, r], sw_recv.at[q, r], other)

    def compute(q, *places):
        for r in places:
            rows0 = pl.multiple_of(lax.rem(z + r, nz) * chunk, 16)
            part[r, :, q * columns : (q + 1) * columns] = mm_nt(buf_ref[pl.ds(rows0, chunk), :], natural[q])
            begin(swap(r, q))

    def term(r, q):
        here = slice(q * columns, (q + 1) * columns)
        return part[r, pl.ds(mine, rows), here] + swapped[r, :, here]

    last = [None, None]

    def ring_step(q, s):
        r = core * (1 + s) + (1 - core) * (nz - 1 - s)
        swap(r, q).wait_recv()
        value = term(r, q)
        if s > 0:
            last[q].wait_recv()
            value = value + ring[s - 1, q]
        acc[s, q] = value
        last[q] = begin(rcopy(acc.at[s, q], ring.at[s, q], ring_send.at[s, q], ring_recv.at[s, q], after))

    pairs = [(r, nz - r) for r in range(1, nz // 2)] + [(nz // 2, 0)]
    load.wait()
    compute(0, *pairs[0])
    compute(0, *pairs[1])
    ring_step(0, 0)
    arrive(coming[1])
    sort(1)
    compute(1, *pairs[0])
    ring_step(0, 1)
    compute(1, *pairs[1])
    ring_step(1, 0)
    for i in range(2, nz // 2):
        compute(0, *pairs[i])
        ring_step(0, i)
        compute(1, *pairs[i])
        ring_step(1, i - 1)
    for i in range(nz // 2, nz - 1):
        ring_step(0, i)
        ring_step(1, i - 1)
    ring_step(1, nz - 2)
    done = []
    for q in range(2):
        swap(0, q).wait_recv()
        value = term(0, q)
        last[q].wait_recv()
        done.append(value + ring[nz - 2, q])
    for j in range(0, 2 * columns, NB):
        k = j // 2
        out_ref[:, j : j + NB] = jnp.concatenate(
            [done[q][:, k + i * share : k + (i + 1) * share] for i in range(NB // 2 // share) for q in range(2)], axis=1
        )
    for copy in pending:
        copy.wait_send()


def project(buffer, share):
    nz = lax.axis_size("tensor") // 2
    n = share.shape[0] * lax.axis_size("dp")
    depth = share.shape[1]
    rows = buffer.shape[0] // nz // 2
    dma = pltpu.SemaphoreType.DMA
    vmem = pl.BlockSpec(memory_space=pltpu.VMEM)
    return pl.pallas_call(
        project_kernel,
        out_shape=jax.ShapeDtypeStruct((rows, n), F32),
        in_specs=[pl.BlockSpec(memory_space=pl.ANY), vmem],
        out_specs=vmem,
        scratch_shapes=[
            pltpu.VMEM(buffer.shape, BF16),
            pltpu.VMEM((2, n // 2, depth), BF16), pltpu.VMEM((2, n // 2, depth), BF16),
            pltpu.VMEM((nz, 2 * rows, n), F32), pltpu.VMEM((nz, rows, n), F32),
            pltpu.VMEM((nz - 1, 2, rows, n // 2), F32), pltpu.VMEM((nz - 1, 2, rows, n // 2), F32),
            dma((1,)),
            dma((2, 2, 4)), dma((2, 2, 4)), dma((2, nz)), dma((2, nz)), dma((nz - 1, 2)), dma((nz - 1, 2)),
        ],
        compiler_params=pltpu.CompilerParams(
            vmem_limit_bytes=58 << 20, collective_id=3, has_side_effects=True
        ),
        cost_estimate=pl.CostEstimate(flops=20_000_000_000, bytes_accessed=16 << 20, transcendentals=0),
        name="project",
    )(buffer, share)


def output_kernel(scale_up, ortho_ref, trans_ref, basis_ref, buf_ref, new_ref, update_ref):
    ortho = ortho_ref[...]
    for k in range(0, trans_ref.shape[0], 512):
        feedback = mm_nt(ortho, trans_ref[k : k + 512, :])
        new_ref[:, k : k + 512] = (buf_ref[:, k : k + 512].astype(F32) - FEEDBACK_SHARE * feedback).astype(BF16)
        product = mm_nt(ortho, basis_ref[k : k + 512, :])
        update_ref[:, k : k + 512] = (-scale_up * product).astype(BF16)


def outputs(ortho, trans, basis, buffer, scale_up):
    rows, depth = buffer.shape
    n = ortho.shape[1]
    tile = rows // 4
    whole = pl.BlockSpec((depth, n), lambda i: (0, 0))
    strip = pl.BlockSpec((tile, depth), lambda i: (i, 0))
    return pl.pallas_call(
        functools.partial(output_kernel, scale_up),
        grid=(rows // tile,),
        out_shape=[jax.ShapeDtypeStruct((rows, depth), BF16)] * 2,
        in_specs=[pl.BlockSpec((tile, n), lambda i: (i, 0)), whole, whole, strip],
        out_specs=[strip, strip],
        compiler_params=pltpu.CompilerParams(vmem_limit_bytes=58 << 20),
        cost_estimate=pl.CostEstimate(flops=8_000_000_000, bytes_accessed=20 << 20, transcendentals=0),
        name="outputs",
    )(ortho, trans, basis, buffer)


def body(buffer, old_basis):
    groups = lax.axis_size("tensor")
    share = old_basis.shape[1]
    rank = share * lax.axis_size("dp")
    projected = project(buffer, old_basis.T)
    ortho_all, trans_all, basis_all = factor(projected, buffer)
    new_basis = lax.dynamic_slice_in_dim(basis_all, lax.axis_index("dp") * share, share, axis=1)
    scale_up = math.sqrt(
        buffer.shape[0] * lax.axis_size("dp") * buffer.shape[1] * groups / rank
    )
    new_buffer, weight_update = outputs(ortho_all, trans_all, basis_all, buffer, scale_up)
    return (new_buffer, weight_update, new_basis)


def solution(mesh):
    in_specs = (P("dp", "tensor"), P("tensor", "dp"))
    out_specs = (P("dp", "tensor"), P("dp", "tensor"), P("tensor", "dp"))
    return jax.shard_map(body, mesh=mesh, in_specs=in_specs, out_specs=out_specs, check_vma=False)
```

```python
import functools
import math

import jax
import jax.numpy as jnp
from jax import lax
from jax.experimental import pallas as pl
from jax.experimental.pallas import tpu as pltpu
from jax.sharding import PartitionSpec as P

NORM_EPS = 1e-06
FEEDBACK_SHARE = 0.05
HI = lax.Precision.HIGHEST
F32 = jnp.float32
BF16 = jnp.bfloat16
NB = 128
MP = 32


def mm_tn(a, b, precision=None):
    return lax.dot_general(
        a, b, (((0,), (0,)), ((), ())), precision=precision, preferred_element_type=F32
    )


def mm_nn(a, b, precision=None):
    return lax.dot_general(
        a, b, (((1,), (0,)), ((), ())), precision=precision, preferred_element_type=F32
    )


def mm_nt(a, b, precision=None):
    return lax.dot_general(
        a, b, (((1,), (1,)), ((), ())), precision=precision, preferred_element_type=F32
    )


def three(x):
    h = x.astype(BF16)
    rest = x - h.astype(F32)
    m = rest.astype(BF16)
    return h, m, (rest - m.astype(F32)).astype(BF16)


def eliminate_rows(rows, r0):
    lane = lax.broadcasted_iota(jnp.int32, (8, NB), 1)
    row = lax.broadcasted_iota(jnp.int32, (8, NB), 0)
    groups = MP // 8
    parts = [rows[8 * g : 8 * g + 8, :] for g in range(groups)]
    cols = [
        [jnp.broadcast_to(parts[g][:, r0 + c : r0 + c + 1], (8, NB)) if g >= c // 8 else None for g in range(groups)]
        for c in range(MP)
    ]
    scales = [jnp.zeros((8, NB), F32) for _ in range(groups)]

    def spread(value, i):
        return jnp.broadcast_to(value[i : i + 1, :], (8, NB))

    for c in range(MP):
        own, at = c // 8, c % 8
        rs = lax.rsqrt(spread(cols[c][own], at))
        inv = rs * rs
        f = [None] * groups
        for g in range(own, groups):
            f[g] = cols[c][g] * inv
        f[own] = jnp.where(row > at, f[own], 0.0)
        for c2 in range(c + 1, MP):
            e = spread(cols[c][c2 // 8], c2 % 8)
            for g in range(c2 // 8, groups):
                cols[c2][g] = cols[c2][g] - f[g] * e
        pivot = jnp.where(lane == r0 + c, 1.0, spread(parts[own], at))
        for g in range(groups):
            if g < own:
                parts[g] = jnp.where(lane == r0 + c, 0.0, parts[g])
            else:
                kept = jnp.where(lane == r0 + c, 0.0, parts[g])
                if g == own:
                    kept = jnp.where(row == at, pivot, kept)
                parts[g] = kept - f[g] * pivot
        scales[own] = jnp.where(row == at, rs, scales[own])
    return jnp.concatenate([p * v for p, v in zip(parts, scales)], axis=0)


def eliminate_block(block):
    lane = lax.broadcasted_iota(jnp.int32, (NB, NB), 1)
    for r0 in range(0, NB, MP):
        rows = eliminate_rows(block[r0 : r0 + MP, :], r0)
        block[r0 : r0 + MP, :] = rows
        if r0 + MP < NB:
            h, m, l = three(rows)
            left = jnp.concatenate([h, h, m, h, l, m], axis=0)
            right = jnp.concatenate([h, m, h, l, h, m], axis=0)
            update = mm_tn(left, right)[r0 + MP :, :]
            below = lane[r0 + MP :, :]
            old = jnp.where((below >= r0) & (below < r0 + MP), 0.0, block[r0 + MP :, :])
            block[r0 + MP :, :] = old - update


def chol_inv(out_ref, block, left, right, between):
    n = out_ref.shape[0]
    nblk = n // NB
    lane = lax.broadcasted_iota(jnp.int32, (NB, NB), 1)
    row = lax.broadcasted_iota(jnp.int32, (NB, NB), 0)

    def step(k, _):
        between(k)
        k0 = pl.multiple_of(k * NB, NB)
        block[...] = out_ref[pl.ds(k0, NB), pl.ds(k0, NB)]
        eliminate_block(block)
        linv = jnp.where(lane <= row, block[...], 0.0)
        out_ref[pl.ds(k0, NB), :] = mm_nn(linv, out_ref[pl.ds(k0, NB), :], HI)
        out_ref[pl.ds(k0, NB), pl.ds(k0, NB)] = linv
        h, m, l = three(out_ref[pl.ds(k0, NB), :])
        for j, (a, b) in enumerate(zip((h, h, m, h, l, m), (h, m, h, l, h, m))):
            left[j * NB : (j + 1) * NB, :] = a
            right[j * NB : (j + 1) * NB, :] = b

        def below(i0, size):
            out_ref[pl.ds(i0, size), pl.ds(k0, NB)] = jnp.zeros((size, NB), F32)
            out_ref[pl.ds(i0, size), :] = out_ref[pl.ds(i0, size), :] - mm_tn(
                left[:, pl.ds(i0, size)], right[...]
            )

        @pl.when(lax.rem(k, 2) == 0)
        def _():
            below(pl.multiple_of(k0 + NB, NB), NB)

        def pair(i, _):
            below(pl.multiple_of(i * 2 * NB, 2 * NB), 2 * NB)
            return 0

        lax.fori_loop(k // 2 + 1, nblk // 2, pair, 0)
        return 0

    lax.fori_loop(0, nblk, step, 0)
    for k0 in range(0, n - NB, NB):
        out_ref[k0 : k0 + NB, k0 + NB :] = jnp.zeros((NB, n - k0 - NB), F32)


def rcopy(src, dst, send_sem, recv_sem, device):
    return pltpu.make_async_remote_copy(
        src_ref=src, dst_ref=dst, send_sem=send_sem, recv_sem=recv_sem,
        device_id=device, device_id_type=pl.DeviceIdType.MESH,
    )


def dp_steps(core):
    dp = lax.axis_index("dp")
    x, y = lax.rem(dp, 4), dp // 4

    def pairs(v):
        gray, high = lax.rem(v + v // 2, 2), v // 2
        near, far = v + 1 - 2 * lax.rem(v, 2), 3 - v
        other = 1 - core
        return (
            (other * near + core * far, other * gray + core * high),
            (other * far + core * near, other * high + core * gray),
        )

    xs = [(y * 4 + v, bit) for v, bit in pairs(x)]
    ys = [(v * 4 + x, bit) for v, bit in pairs(y)]
    return (xs + ys, ys + xs)


def enter(devices):
    barrier = pltpu.get_barrier_semaphore()
    for device in devices:
        pl.semaphore_signal(barrier, inc=1, device_id=device, device_id_type=pl.DeviceIdType.MESH)
    pl.semaphore_wait(barrier, len(devices))


def dp_offsets(dp, core, length):
    def bits(v):
        gray, high = (v + v // 2) % 2, v // 2
        other = 1 - core
        return [other * gray + core * high, other * high + core * gray]

    xs, ys = bits(dp % 4), bits(dp // 4)
    out = []
    for order in (xs + ys, ys + xs):
        at, size = 0, length
        for bit in order:
            size //= 2
            at = at + bit * size
        out.append(at)
    return out


def factor_kernel(
    p_ref, buf_hbm, ortho_hbm, trans_ref, basis_ref, buf_ref, ortho_ref, inv_ref, all_ref, left, right, inv_hi, inv_lo, stacked, part, half, got, sums, zgot, zsums, whole, block, mixed, mixed_got, sq, sq_t, sq_d, sq_sum, core_send, core_recv, dp_send, dp_recv, z_send, z_recv, ag_send, ag_recv, zag_send, zag_recv, plus_send, plus_recv, minus_send, minus_recv, pair_send, pair_recv, w_send, w_recv, tr_send, tr_recv, t_send, t_recv, d_send, d_recv, local_sem,
):
    dp, tensor = lax.axis_index("dp"), lax.axis_index("tensor")
    core, z = lax.rem(tensor, 2), tensor // 2
    nz = lax.axis_size("tensor") // 2
    other = (dp, tensor + 1 - 2 * core)
    steps = dp_steps(core)
    ndp, ntensor = lax.axis_size("dp"), 2 * nz
    zdev = [(dp, lax.rem(z + d, nz) * 2 + core) for d in range(nz)]
    tdev = [(dp, lax.rem(tensor + d, ntensor)) for d in range(ntensor)]
    ddev = [(lax.rem(dp + d, ndp), tensor) for d in range(ndp)]
    load = pltpu.make_async_copy(buf_hbm, buf_ref, local_sem.at[0])
    load.start()
    enter(tdev[1:] + ddev[1:])
    pending = []

    prows, n = p_ref.shape

    places = [lax.rem(z + (1 - 2 * core) * r + nz, nz) for r in range(nz)]
    ahead, behind = [(dp, places[r] * 2 + core) for r in (1, nz - 1)]

    own_at = [pl.multiple_of((places[r] * 2 + core) * prows, 8) for r in range(nz)]

    def region(r):
        return all_ref.at[pl.ds(own_at[r], prows)]

    def begin(copy):
        copy.start()
        pending.append(copy)
        return copy

    def pass_on(j):
        plus = region(nz - j if j else 0)
        begin(rcopy(plus, plus, plus_send.at[j], plus_recv.at[j], ahead))
        if j < nz // 2 - 1:
            minus = region(j)
            begin(rcopy(minus, minus, minus_send.at[j], minus_recv.at[j], behind))

    def pair_copy(r):
        here = region(r)
        return rcopy(here, here, pair_send.at[r], pair_recv.at[r], other)

    def across(r):
        pair_copy(r).start()

    def poll(j):
        here = region(nz - j)
        rcopy(here, here, plus_send.at[j - 1], plus_recv.at[j - 1], ahead).wait_recv()
        if j < nz // 2:
            here = region(j)
            rcopy(here, here, minus_send.at[j - 1], minus_recv.at[j - 1], behind).wait_recv()
            pass_on(j)
            across(j)
        across(nz - j)

    chunk = 2 * prows
    chunk_at = [pl.multiple_of(places[r] * chunk, 16) for r in range(nz)]

    def accumulate(r):
        here = region(r)
        rcopy(here, here, pair_send.at[r], pair_recv.at[(nz - r) % nz], other).wait_recv()
        rows0 = chunk_at[r]
        wide = all_ref[pl.ds(rows0, chunk), :]
        high = wide.astype(BF16)
        low = (wide - high.astype(F32)).astype(BF16)

        for i0 in range(0, mixed.shape[0], 256):
            columns = buf_ref[pl.ds(rows0, chunk), i0 : i0 + 256]
            for k in range(0, n, 256):
                value = mm_tn(columns, high[:, k : k + 256]) + mm_tn(columns, low[:, k : k + 256])
                if r:
                    value = value + mixed[i0 : i0 + 256, k : k + 256]
                mixed[i0 : i0 + 256, k : k + 256] = value

    own_rows = pl.multiple_of(tensor * prows, 8)
    all_ref[pl.ds(own_rows, prows), :] = p_ref[...]
    pass_on(0)
    across(0)

    nblk = n // NB
    order = [[0, 1, nblk - 2, nblk - 1], list(range(2, nblk - 2))]
    spots = {}
    for i in order[0] + order[1]:
        for j in range(i, nblk):
            spots[i, j] = len(spots) * NB
    rows = len(spots) * NB // 2
    mine = pl.multiple_of(core * rows, 8)
    theirs = pl.multiple_of((1 - core) * rows, 8)
    deep = -(-prows // 16) * 16
    padded = jnp.concatenate([p_ref[...], jnp.zeros((deep - prows, n), F32)], axis=0)
    h, m, l = three(padded)
    for j, (a, b) in enumerate(zip((h, h, m, h, l, m), (h, m, h, l, h, m))):
        left[j * deep : (j + 1) * deep, :] = a
        right[j * deep : (j + 1) * deep, :] = b

    def gram_half(which):
        for i in order[which][::2]:
            i0 = i * NB
            prod = mm_tn(left[0 : 6 * deep, i0 : i0 + 2 * NB], right[0 : 6 * deep, i0:])
            for i2 in (i, i + 1):
                for j in range(i2, nblk):
                    at = spots[i2, j]
                    part[at : at + NB, :] = prod[(i2 - i) * NB : (i2 - i + 1) * NB, (j - i) * NB : (j - i + 1) * NB]

    for c in range(2):
        @pl.when(core == c)
        def _():
            gram_half(1 - c)

    swap = begin(rcopy(part.at[pl.ds(theirs, rows)], half, core_send.at[0, 0], core_recv.at[0, 0], other))
    for c in range(2):
        @pl.when(core == c)
        def _():
            gram_half(c)

    swap.wait_recv()
    half[...] = half[...] + part[pl.ds(mine, rows), :]

    length = rows // 2
    offs = [0, length]
    trail = []
    size = length
    got_at = 0
    for k in range(4):
        size //= 2
        copies = []
        for s in range(2):
            partner, bit = steps[s][k]
            keep = pl.multiple_of(offs[s] + bit * size, 8)
            give = pl.multiple_of(offs[s] + (1 - bit) * size, 8)
            copies.append(begin(rcopy(half.at[pl.ds(give, size)], got.at[s, pl.ds(got_at, size)], dp_send.at[s, k], dp_recv.at[s, k], (partner, tensor))))
            offs[s] = keep
        if k == 0:
            load.wait()
            accumulate(0)
        for s in range(2):
            copies[s].wait_recv()
            half[pl.ds(offs[s], size), :] = half[pl.ds(offs[s], size), :] + got[s, pl.ds(got_at, size), :]
        if k == 0:
            poll(1)
        trail.append((size, list(offs)))
        got_at += size

    sums[0:size, :] = half[pl.ds(offs[0], size), :]
    sums[size : 2 * size, :] = half[pl.ds(offs[1], size), :]
    piece = sums.shape[0] // nz
    if sums.shape[0] > 2 * size:
        sums[2 * size :, :] = jnp.zeros((sums.shape[0] - 2 * size, NB), F32)
    copies = []
    for d in range(1, nz):
        zto = lax.rem(z + d, nz)
        copies.append(begin(rcopy(sums.at[pl.ds(pl.multiple_of(zto * piece, 8), piece)], zgot.at[d], z_send.at[d], z_recv.at[d], zdev[d])))
    own = pl.multiple_of(z * piece, 8)
    total = sums[pl.ds(own, piece), :]
    for d in range(1, nz):
        copies[d - 1].wait_recv()
        total = total + zgot[d]
    zsums[pl.ds(own, piece), :] = total
    copies = []
    for d in range(1, nz):
        copies.append(begin(rcopy(zsums.at[pl.ds(own, piece)], zsums.at[pl.ds(own, piece)], zag_send.at[d], zag_recv.at[d], zdev[d])))
    for copy in copies:
        copy.wait_recv()
    poll(2)

    def to_other(stage, s, start, count):
        here = whole.at[pl.ds(pl.multiple_of(mine + start, 8), count)]
        return begin(rcopy(here, here, core_send.at[s, stage], core_recv.at[s, stage], other))

    passed = []
    for s in range(2):
        whole[pl.ds(pl.multiple_of(mine + offs[s], 8), size), :] = zsums[s * size : (s + 1) * size, :]
        passed.append(to_other(1, s, offs[s], size))
    for k in reversed(range(4)):
        size, offs = trail[k]
        copies = []
        for s in range(2):
            here = whole.at[pl.ds(pl.multiple_of(mine + offs[s], 8), size)]
            copies.append(begin(rcopy(here, here, ag_send.at[s, k], ag_recv.at[s, k], (steps[s][k][0], tensor))))
        if k == 3:
            accumulate(1)
        elif k == 2:
            accumulate(nz - 1)
        elif k == 0:
            poll(3)
            accumulate(2)
            accumulate(nz - 2)
        for s in range(2):
            copies[s].wait_recv()
            passed.append(to_other(5 - k, s, offs[s] + (1 - 2 * steps[s][k][1]) * size, size))
    accumulate(3)
    accumulate(nz - 3)
    for copy in passed:
        copy.wait_recv()

    wlen = mixed.shape[0] // 2
    woffs = dp_offsets(dp, core, wlen)

    def mixed_copy(k, s):
        size = wlen >> (k + 1)
        partner, bit = steps[s][k]
        keep = s * wlen + woffs[s] // size * size
        give = keep + (1 - 2 * bit) * size
        slot = mixed_got.at[s, pl.ds(wlen - 2 * size, size)]
        return rcopy(mixed.at[pl.ds(pl.multiple_of(give, 8), size)], slot, w_send.at[s, k], w_recv.at[s, k], (partner, tensor)), keep, size

    def mixed_add(k):
        for s in range(2):
            copy, keep, size = mixed_copy(k, s)
            copy.wait_recv()
            rows = pl.ds(pl.multiple_of(keep, 8), size)
            mixed[rows, :] = mixed[rows, :] + mixed_got[s, wlen - 2 * size : wlen - size, :]

    def mixed_send(k):
        for s in range(2):
            mixed_copy(k, s)[0].start()

    for i in range(nblk):
        for j in range(nblk):
            if j < i:
                value = jnp.zeros((NB, NB), F32)
            else:
                value = whole[spots[i, j] : spots[i, j] + NB, :]
            inv_ref[i * NB : (i + 1) * NB, j * NB : (j + 1) * NB] = value

    def between(k):
        @pl.when(k == 1)
        def _():
            poll(nz // 2)
            accumulate(nz // 2)
            mixed_send(0)

        for phase, at in enumerate((4, 6, 7)):
            @pl.when(k == at)
            def _():
                mixed_add(phase)
                mixed_send(phase + 1)

    chol_inv(inv_ref, block, left, right, between)

    for k in range(0, n, 256):
        wide = inv_ref[k : k + 256, 0 : k + 256]
        high = wide.astype(BF16)
        inv_hi[k : k + 256, 0 : k + 256] = high
        inv_lo[k : k + 256, 0 : k + 256] = (wide - high.astype(F32)).astype(BF16)
    mixed_add(3)
    piece = wlen >> 4
    share = 2 * piece
    rows_at = [pl.multiple_of(s * wlen + woffs[s], 16) for s in range(2)]
    for s in range(2):
        wide = mixed[pl.ds(rows_at[s], piece), :]
        high = wide.astype(BF16)
        stacked[s * piece : (s + 1) * piece, :] = high
        stacked[share + s * piece : share + (s + 1) * piece, :] = (wide - high.astype(F32)).astype(BF16)
    def trans_part(k):
        e = k + 256
        both = mm_nt(stacked[:, 0:e], inv_hi[k:e, 0:e])
        trans = both[0:share, :] + both[share:, :] + mm_nt(stacked[0:share, 0:e], inv_lo[k:e, 0:e])
        squares = jnp.sum(trans * trans, axis=0, keepdims=True)
        for j in range(0, 256, NB):
            sq[(k + j) // NB : (k + j) // NB + 1, :] = squares[:, j : j + NB]
        half_part = trans.astype(BF16)
        for s in range(2):
            trans_ref[pl.ds(rows_at[s], piece), k:e] = half_part[s * piece : (s + 1) * piece, :]

    def gather_step(q, k):
        size = wlen >> (k + 1)
        copies = []
        for s in range(2):
            start = s * wlen + woffs[s] // size * size
            here = trans_ref.at[pl.ds(pl.multiple_of(start, 16), size), pl.ds(q * n // 2, n // 2)]
            copies.append(begin(rcopy(here, here, tr_send.at[q, s, k], tr_recv.at[q, s, k], (steps[s][k][0], tensor))))
        return copies

    def spread(source, slots, send, recv, devices):
        copies = []
        for d in range(1, len(devices)):
            copies.append(begin(rcopy(source, slots.at[d], send.at[d], recv.at[d], devices[d])))
        return copies

    def sum_of(source, slots, copies):
        out = source[...]
        for d in range(1, slots.shape[0]):
            copies[d - 1].wait_recv()
            out = out + slots[d]
        return out

    stores = []

    def ortho_part(i):
        count = all_ref.shape[0] // 4
        rows0 = i * count
        wide = all_ref[rows0 : rows0 + count, :]
        high = wide.astype(BF16)
        low = (wide - high.astype(F32)).astype(BF16)
        for k in range(0, n, 256):
            e = k + 256
            hi, lo = inv_hi[k:e, 0:e], inv_lo[k:e, 0:e]
            value = mm_nt(high[:, 0:e], hi) + (mm_nt(low[:, 0:e], hi) + mm_nt(high[:, 0:e], lo))
            ortho_ref[rows0 : rows0 + count, k:e] = value.astype(BF16)
        here = pl.ds(rows0, count)
        store = pltpu.make_async_copy(ortho_ref.at[here], ortho_hbm.at[here], local_sem.at[1 + i])
        store.start()
        stores.append(store)

    trans_part(0)
    trans_part(256)
    coming = [gather_step(0, 3)]
    trans_part(512)
    trans_part(768)
    coming.append(gather_step(1, 3))
    beside = spread(sq, sq_t, t_send, t_recv, tdev)
    for i, k in enumerate((2, 1, 0)):
        ortho_part(i)
        for q in range(2):
            for copy in coming[q]:
                copy.wait_recv()
            coming[q] = gather_step(q, k)
        if i == 0:
            sq_sum[...] = sum_of(sq, sq_t, beside)
            down = spread(sq_sum, sq_d, d_send, d_recv, ddev)
    ortho_part(3)
    scale = lax.rsqrt(sum_of(sq_sum, sq_d, down) + NORM_EPS)
    for q in range(2):
        for copy in coming[q]:
            copy.wait_recv()
        for rows0 in range(0, trans_ref.shape[0], NB):
            for j in range(q * nblk // 2, (q + 1) * nblk // 2):
                value = trans_ref[rows0 : rows0 + NB, j * NB : (j + 1) * NB].astype(F32)
                basis_ref[rows0 : rows0 + NB, j * NB : (j + 1) * NB] = (value * scale[j : j + 1, :]).astype(BF16)
    for k in range(4):
        for s in range(2):
            mixed_copy(k, s)[0].wait_send()
    for store in stores:
        store.wait()
    for r in range(nz):
        pair_copy(r).wait_send()
    for copy in pending:
        copy.wait_send()


def factor(projected, buffer):
    prows, n = projected.shape
    depth = buffer.shape[1]
    nblk = n // NB
    packed = nblk * (nblk + 1) // 2 * NB
    ntensor, ndp = lax.axis_size("tensor"), lax.axis_size("dp")
    nz = ntensor // 2
    rows = packed // 2
    last = rows // 2 // 16
    piece = -(-2 * last // (8 * nz)) * 8
    dma = pltpu.SemaphoreType.DMA
    vmem = pl.BlockSpec(memory_space=pltpu.VMEM)

    def f32(*shape):
        return pltpu.VMEM(shape, F32)

    def bf16(*shape):
        return pltpu.VMEM(shape, BF16)

    return pl.pallas_call(
        factor_kernel,
        out_shape=[
            jax.ShapeDtypeStruct((prows * ntensor, n), BF16),
            jax.ShapeDtypeStruct((depth, n), BF16),
            jax.ShapeDtypeStruct((depth, n), BF16),
        ],
        in_specs=[vmem, pl.BlockSpec(memory_space=pl.ANY)],
        out_specs=[pl.BlockSpec(memory_space=pl.ANY), vmem, vmem],
        scratch_shapes=[
            bf16(*buffer.shape), bf16(prows * ntensor, n), f32(n, n), f32(prows * ntensor, n), bf16(6 * NB, n), bf16(6 * NB, n),
            bf16(n, n), bf16(n, n), bf16(2 * depth // ndp, n),
            f32(packed, NB), f32(rows, NB), f32(2, rows // 2, NB),
            f32(piece * nz, NB), f32(nz, piece, NB), f32(piece * nz, NB), f32(packed, NB),
            f32(NB, NB), f32(depth, n), f32(2, depth // 2, n),
            f32(nblk, NB), f32(ntensor, nblk, NB), f32(ndp, nblk, NB), f32(nblk, NB),
            dma((2, 6)), dma((2, 6)), dma((2, 4)), dma((2, 4)), dma((nz,)), dma((nz,)),
            dma((2, 4)), dma((2, 4)), dma((nz,)), dma((nz,)),
            dma((nz // 2,)), dma((nz // 2,)), dma((nz // 2,)), dma((nz // 2,)), dma((nz,)), dma((nz,)),
            dma((2, 4)), dma((2, 4)), dma((2, 2, 4)), dma((2, 2, 4)),
            dma((ntensor,)), dma((ntensor,)), dma((ndp,)), dma((ndp,)), dma((5,)),
        ],
        compiler_params=pltpu.CompilerParams(
            vmem_limit_bytes=58 << 20, collective_id=1, has_side_effects=True
        ),
        cost_estimate=pl.CostEstimate(flops=60_000_000_000, bytes_accessed=24 << 20, transcendentals=0),
        name="factor",
    )(projected, buffer)


def project_kernel(buf_hbm, share_ref, out_ref, buf_ref, basis, natural, part, swapped, acc, ring, load_sem, ag_send, ag_recv, sw_send, sw_recv, ring_send, ring_recv):
    dp, tensor = lax.axis_index("dp"), lax.axis_index("tensor")
    ndp, nz = lax.axis_size("dp"), lax.axis_size("tensor") // 2
    core, z = lax.rem(tensor, 2), tensor // 2
    other = (dp, tensor + 1 - 2 * core)
    after = (dp, lax.rem(z + 1 - 2 * core + nz, nz) * 2 + core)
    before = (dp, lax.rem(z - 1 + 2 * core + nz, nz) * 2 + core)
    steps = dp_steps(core)
    load = pltpu.make_async_copy(buf_hbm, buf_ref, load_sem.at[0])
    load.start()
    enter([(partner, tensor) for partner, _ in steps[0]] + [other, after, before])
    pending = []

    def begin(copy):
        copy.start()
        pending.append(copy)
        return copy

    share = share_ref.shape[0] // 2
    length = basis.shape[1] // 2
    offs = dp_offsets(dp, core, length)
    half = share // 2
    for q in range(2):
        for s in range(2):
            basis[q, pl.ds(pl.multiple_of(s * length + offs[s], 16), half), :] = share_ref[
                q * share + s * half : q * share + (s + 1) * half, :
            ]

    def gather_step(q, k):
        size = length >> (k + 1)
        copies = []
        for s in range(2):
            here = basis.at[q, pl.ds(pl.multiple_of(s * length + offs[s] // size * size, 16), size)]
            copies.append(begin(rcopy(here, here, ag_send.at[q, s, k], ag_recv.at[q, s, k], (steps[s][k][0], tensor))))
        return copies

    def arrive(copies):
        for copy in copies:
            copy.wait_recv()

    def sort(q):
        for d in range(ndp):
            there = dp_offsets(d, core, length)
            for s in range(2):
                rows0 = d * share + s * half
                natural[q, rows0 : rows0 + half, :] = basis[q, pl.ds(pl.multiple_of(s * length + there[s], 16), half), :]

    coming = [gather_step(q, 3) for q in range(2)]
    for k in (2, 1, 0):
        for q in range(2):
            arrive(coming[q])
            coming[q] = gather_step(q, k)
    arrive(coming[0])
    sort(0)

    chunk = buf_ref.shape[0] // nz
    rows = chunk // 2
    mine = pl.multiple_of(core * rows, 8)
    theirs = pl.multiple_of((1 - core) * rows, 8)
    columns = out_ref.shape[1] // 2

    def swap(r, q):
        here = pl.ds(q * columns, columns)
        return rcopy(part.at[r, pl.ds(theirs, rows), here], swapped.at[r, :, here], sw_send.at[q, r], sw_recv.at[q, r], other)

    def compute(q, *places):
        for r in places:
            rows0 = pl.multiple_of(lax.rem(z + r, nz) * chunk, 16)
            part[r, :, q * columns : (q + 1) * columns] = mm_nt(buf_ref[pl.ds(rows0, chunk), :], natural[q])
            begin(swap(r, q))

    def term(r, q):
        here = slice(q * columns, (q + 1) * columns)
        return part[r, pl.ds(mine, rows), here] + swapped[r, :, here]

    last = [None, None]

    def ring_step(q, s):
        r = core * (1 + s) + (1 - core) * (nz - 1 - s)
        swap(r, q).wait_recv()
        value = term(r, q)
        if s > 0:
            last[q].wait_recv()
            value = value + ring[s - 1, q]
        acc[s, q] = value
        last[q] = begin(rcopy(acc.at[s, q], ring.at[s, q], ring_send.at[s, q], ring_recv.at[s, q], after))

    pairs = [(r, nz - r) for r in range(1, nz // 2)] + [(nz // 2, 0)]
    load.wait()
    compute(0, *pairs[0])
    compute(0, *pairs[1])
    ring_step(0, 0)
    arrive(coming[1])
    sort(1)
    compute(1, *pairs[0])
    ring_step(0, 1)
    compute(1, *pairs[1])
    ring_step(1, 0)
    for i in range(2, nz // 2):
        compute(0, *pairs[i])
        ring_step(0, i)
        compute(1, *pairs[i])
        ring_step(1, i - 1)
    for i in range(nz // 2, nz - 1):
        ring_step(0, i)
        ring_step(1, i - 1)
    ring_step(1, nz - 2)
    done = []
    for q in range(2):
        swap(0, q).wait_recv()
        value = term(0, q)
        last[q].wait_recv()
        done.append(value + ring[nz - 2, q])
    for j in range(0, 2 * columns, NB):
        k = j // 2
        out_ref[:, j : j + NB] = jnp.concatenate(
            [done[q][:, k + i * share : k + (i + 1) * share] for i in range(NB // 2 // share) for q in range(2)], axis=1
        )
    for copy in pending:
        copy.wait_send()


def project(buffer, share):
    nz = lax.axis_size("tensor") // 2
    n = share.shape[0] * lax.axis_size("dp")
    depth = share.shape[1]
    rows = buffer.shape[0] // nz // 2
    dma = pltpu.SemaphoreType.DMA
    vmem = pl.BlockSpec(memory_space=pltpu.VMEM)
    return pl.pallas_call(
        project_kernel,
        out_shape=jax.ShapeDtypeStruct((rows, n), F32),
        in_specs=[pl.BlockSpec(memory_space=pl.ANY), vmem],
        out_specs=vmem,
        scratch_shapes=[
            pltpu.VMEM(buffer.shape, BF16),
            pltpu.VMEM((2, n // 2, depth), BF16), pltpu.VMEM((2, n // 2, depth), BF16),
            pltpu.VMEM((nz, 2 * rows, n), F32), pltpu.VMEM((nz, rows, n), F32),
            pltpu.VMEM((nz - 1, 2, rows, n // 2), F32), pltpu.VMEM((nz - 1, 2, rows, n // 2), F32),
            dma((1,)),
            dma((2, 2, 4)), dma((2, 2, 4)), dma((2, nz)), dma((2, nz)), dma((nz - 1, 2)), dma((nz - 1, 2)),
        ],
        compiler_params=pltpu.CompilerParams(
            vmem_limit_bytes=58 << 20, collective_id=3, has_side_effects=True
        ),
        cost_estimate=pl.CostEstimate(flops=20_000_000_000, bytes_accessed=16 << 20, transcendentals=0),
        name="project",
    )(buffer, share)


def output_kernel(scale_up, ortho_ref, trans_ref, basis_ref, buf_ref, new_ref, update_ref):
    ortho = ortho_ref[...]
    for k in range(0, trans_ref.shape[0], 512):
        feedback = mm_nt(ortho, trans_ref[k : k + 512, :])
        new_ref[:, k : k + 512] = (buf_ref[:, k : k + 512].astype(F32) - FEEDBACK_SHARE * feedback).astype(BF16)
        product = mm_nt(ortho, basis_ref[k : k + 512, :])
        update_ref[:, k : k + 512] = (-scale_up * product).astype(BF16)


def outputs(ortho, trans, basis, buffer, scale_up):
    rows, depth = buffer.shape
    n = ortho.shape[1]
    tile = rows // 4
    whole = pl.BlockSpec((depth, n), lambda i: (0, 0))
    strip = pl.BlockSpec((tile, depth), lambda i: (i, 0))
    return pl.pallas_call(
        functools.partial(output_kernel, scale_up),
        grid=(rows // tile,),
        out_shape=[jax.ShapeDtypeStruct((rows, depth), BF16)] * 2,
        in_specs=[pl.BlockSpec((tile, n), lambda i: (i, 0)), whole, whole, strip],
        out_specs=[strip, strip],
        compiler_params=pltpu.CompilerParams(vmem_limit_bytes=58 << 20),
        cost_estimate=pl.CostEstimate(flops=8_000_000_000, bytes_accessed=20 << 20, transcendentals=0),
        name="outputs",
    )(ortho, trans, basis, buffer)


def body(buffer, old_basis):
    groups = lax.axis_size("tensor")
    share = old_basis.shape[1]
    rank = share * lax.axis_size("dp")
    projected = project(buffer, old_basis.T)
    ortho_all, trans_all, basis_all = factor(projected, buffer)
    new_basis = lax.dynamic_slice_in_dim(basis_all, lax.axis_index("dp") * share, share, axis=1)
    scale_up = math.sqrt(
        buffer.shape[0] * lax.axis_size("dp") * buffer.shape[1] * groups / rank
    )
    new_buffer, weight_update = outputs(ortho_all, trans_all, basis_all, buffer, scale_up)
    return (new_buffer, weight_update, new_basis)


def solution(mesh):
    in_specs = (P("dp", "tensor"), P("tensor", "dp"))
    out_specs = (P("dp", "tensor"), P("dp", "tensor"), P("tensor", "dp"))
    return jax.shard_map(body, mesh=mesh, in_specs=in_specs, out_specs=out_specs, check_vma=False)
```
